256 devices in a mesh: bead: 16 (over x_hi, z), space: 16 (over x_lo, y, core).
Axes of the slice: x: 4 (x_hi: 2, x_lo: 2; x = x_hi * 2 + x_lo), y: 4, z: 8, core: 2. Of those that a mesh axis runs over, the one named last changes fastest.
Arguments:
- coords: float32 [32, 3, 4096], P('bead', None, 'space'), may hold values from -6 to 6
- momenta: float32 [32, 3, 4096], P('bead', None, 'space'), may hold values from -12 to 12
- species: int32 [4096], P('space'), may hold values from 0 to 4
- atom_features: float32 [4096, 128], P('space'), may hold values from -4 to 4
- neighbours: int32 [32, 4096, 16], P('bead', 'space'), may hold values from -1 to 511, as said below
- ghost_rows: int32 [32, 4096], P('bead', 'space'), may hold values from 0 to 255
- embed: float32 [5, 128], replicated, may hold values from -5 to 5
- w_filter: float32 [2, 16, 128], replicated, may hold values from -1.5 to 1.5
- w_value: bfloat16 [2, 128, 128], replicated, may hold values from -0.5 to 0.5
- w_out: bfloat16 [2, 128, 128], replicated, may hold values from -0.5 to 0.5
- readout: float32 [128], replicated, may hold values from -0.5 to 0.5
Outputs:
- new_coords: float32 [32, 3, 4096], P('bead', None, 'space')
- new_momenta: float32 [32, 3, 4096], P('bead', None, 'space')
The draws below stay inside these ranges and needn't reach their ends.
Inputs may be any that keep to these rules, and one draw needn't show every extreme that they name: `neighbours`: each entry is -1 (empty slot) or an index into the domain's extended numbering: 256 own atoms, then 128 atoms from the domain on the left, then 128 from the domain on the right. `ghost_rows`: entries are own-atom indices of the domain; in a domain's block of 256, the first half goes to the domain on its left, the second half to the one on its right; the domains form a closed cycle.
All inputs are finite; a program needn't handle non-finite values.
Results may differ from the reference program's by a relative error of at most 0.015.
Values may be sent and summed in bfloat16 or wider, within the bound.
A program may use at most 64 MiB of HBM per device.

```python
import math
import jax
import jax.numpy as jnp
from jax import lax

C = 128
NB = 16
K = 16
SPECIES = 5
LAYERS = 2
A_DEV = 256
GHOST = 128
BEADS = 32
ATOMS = 4096
N_SPACE = 16


def draw_neighbours(key, part):
    key = jax.random.fold_in(key, 11)
    index_key, empty_key = jax.random.split(key)
    picks = jax.random.randint(index_key, (BEADS, ATOMS, K), 0, A_DEV + 2 * GHOST)
    empty = jax.random.randint(empty_key, (BEADS, ATOMS, K), 0, 4)
    return jnp.where(empty == 0, -1, picks).astype(jnp.int32)


def touch_ends(drawn, own_key, smallest, top_value):
    dims = drawn.shape
    place = [jax.random.randint(jax.random.fold_in(own_key, axis), (), 0, dims[axis]) for axis in range(len(dims))]
    drawn = drawn.at[tuple(place)].set(smallest)
    longest = dims.index(max(dims))
    place[longest] = (place[longest] + 1) % dims[longest]
    return drawn.at[tuple(place)].set(top_value)


def block_scale(own_key, extent, cuts, least, high):
    level = 1.0
    for dim, blocks in cuts:
        heights = jax.random.uniform(jax.random.fold_in(jax.random.fold_in(own_key, 6), dim), (blocks,), jnp.float32, least / len(cuts), high / len(cuts))
        level = level * jnp.repeat(jnp.exp(heights), extent[dim] // blocks).reshape((-1,) + (1,) * (len(extent) - 1 - dim))
    return level


def normal_values(rng, dims, width, most, cuts=(), held_as=jnp.bfloat16):
    values = width * jax.random.normal(rng, dims, jnp.float32)
    if cuts:
        values = values * block_scale(rng, dims, cuts, -0.22, 0.18)
    return jnp.clip(values, -most, most).astype(held_as)


def setup_inputs(seed: int = 0) -> dict:
    key_of = jax.random.split(jax.random.key(seed), 12)
    coords = normal_values(key_of[0], (BEADS, 3, ATOMS), 1.0, 6.0, ((0, 16), (2, 16)), jnp.float32)
    momenta = normal_values(key_of[1], (BEADS, 3, ATOMS), 2.0, 12.0, ((0, 16), (2, 16)), jnp.float32)
    species = touch_ends(jax.random.randint(key_of[2], (ATOMS,), 0, SPECIES), jax.random.fold_in(key_of[2], 1), 0, SPECIES - 1).astype(jnp.int32)
    atom_features = normal_values(key_of[3], (ATOMS, C), 0.7, 4.0, ((0, 16),), jnp.float32)
    neighbours = draw_neighbours(jax.random.fold_in(key_of[11], 71), 0)
    ghost_rows = touch_ends(jax.random.randint(key_of[5], (BEADS, 2 * GHOST * N_SPACE), 0, A_DEV), jax.random.fold_in(key_of[5], 1), 0, A_DEV - 1).astype(jnp.int32)
    embed = normal_values(key_of[6], (SPECIES, C), 1.0, 5.0, (), jnp.float32)
    w_filter = normal_values(key_of[7], (LAYERS, NB, C), NB ** -0.5, 1.5, (), jnp.float32)
    w_value = normal_values(key_of[8], (LAYERS, C, C), C ** -0.5, 0.5)
    w_out = normal_values(key_of[9], (LAYERS, C, C), C ** -0.5, 0.5)
    readout = normal_values(key_of[10], (C,), C ** -0.5, 0.5, (), jnp.float32)
    return dict(coords=coords, momenta=momenta, species=species, atom_features=atom_features, neighbours=neighbours, ghost_rows=ghost_rows, embed=embed, w_filter=w_filter, w_value=w_value, w_out=w_out, readout=readout)


MASSES = (1.008, 12.011, 14.007, 15.999, 30.974)
STEP_DT = 1.0
OMEGA_P = 0.6
WIDTH = 3.125
SPACING = 0.25
SOFTEN = 0.01

def value_rows(hidden, weight):
    shape = hidden.shape
    flat = hidden.astype(jnp.bfloat16).reshape(-1, shape[-1])
    return jnp.dot(flat, weight, preferred_element_type=jnp.float32).reshape(shape[:-1] + (weight.shape[1],))

def mix_layer(hidden, message, weight):
    shape = message.shape
    flat = message.astype(jnp.bfloat16).reshape(-1, shape[-1])
    update = jnp.dot(flat, weight, preferred_element_type=jnp.float32).reshape(shape)
    return hidden + jax.nn.silu(update)

def edge_messages(values, positions, lists, w_radial):
    own_count = lists.shape[1]
    clipped = jnp.maximum(lists, 0)
    present = (lists >= 0).astype(jnp.float32)
    own_xyz = positions[:, :, :own_count]
    far_xyz = jax.vmap(lambda xe, ix: xe[:, ix])(positions, clipped)
    offset = far_xyz - own_xyz[:, :, :, None]
    distance = jnp.sqrt(lax.optimization_barrier(jnp.sum(offset * offset, axis=1)) + SOFTEN)
    centers = SPACING * jnp.arange(w_radial.shape[0], dtype=jnp.float32)
    radial = jnp.exp(-WIDTH * (distance[..., None] - centers) ** 2)
    filters = jnp.einsum('bakn,nc->bakc', radial, w_radial, precision=lax.Precision.HIGHEST)
    far_values = jax.vmap(lambda v, ix: v[ix])(values, clipped)
    return lax.optimization_barrier(jnp.sum(filters * far_values * present[..., None], axis=2))

def normal_table(count):
    j_index = jnp.arange(count, dtype=jnp.float32)[:, None]
    k_index = jnp.arange(count, dtype=jnp.float32)[None, :]
    angle = 2.0 * math.pi * j_index * k_index / count
    border = (k_index == 0.0) | (k_index == float(count // 2))
    inner = jnp.where(k_index < count / 2.0, jnp.cos(angle), jnp.sin(angle)) * math.sqrt(2.0 / count)
    matrix = jnp.where(border, jnp.cos(angle) / math.sqrt(count), inner)
    omegas = 2.0 * OMEGA_P * jnp.sin(math.pi * jnp.arange(count, dtype=jnp.float32) / count)
    return (matrix, omegas)

def advance(normal_modes, omegas, masses):
    positions_m = normal_modes[:, :3]
    momenta_m = normal_modes[:, 3:]
    freq = omegas[:, None, None]
    guarded = jnp.where(freq > 0.0, freq, 1.0)
    cosine = jnp.cos(freq * STEP_DT)
    sine_term = jnp.sin(freq * STEP_DT)
    drift_term = jnp.where(freq > 0.0, sine_term / guarded, STEP_DT)
    new_positions = cosine * positions_m + drift_term * momenta_m / masses
    new_momenta = cosine * momenta_m - masses * freq * sine_term * positions_m
    return jnp.concatenate([new_positions, new_momenta], axis=1)

def global_lists(neighbours, ghost_rows):
    blocks = ghost_rows.reshape(BEADS, N_SPACE, 2 * GHOST)
    offsets = (jnp.arange(N_SPACE, dtype=jnp.int32) * A_DEV)[None, :, None]
    own_rows = jnp.broadcast_to(offsets + jnp.arange(A_DEV, dtype=jnp.int32)[None, None, :], (BEADS, N_SPACE, A_DEV))
    left_rows = jnp.roll(blocks[:, :, GHOST:] + offsets, 1, axis=1)
    right_rows = jnp.roll(blocks[:, :, :GHOST] + offsets, -1, axis=1)
    numbering = jnp.concatenate([own_rows, left_rows, right_rows], axis=2).astype(jnp.int32)
    local_lists = neighbours.reshape(BEADS, N_SPACE, A_DEV * K)
    located = jnp.take_along_axis(numbering, jnp.maximum(local_lists, 0).astype(jnp.int32), axis=2)
    return jnp.where(local_lists >= 0, located, -1).astype(jnp.int32).reshape(BEADS, ATOMS, K)

def reference(coords, momenta, species, atom_features, neighbours, ghost_rows, embed, w_filter, w_value, w_out, readout):
    onehot = (species[:, None] == jnp.arange(SPECIES, dtype=jnp.int32)[None, :]).astype(jnp.float32)
    h_start = jnp.dot(onehot, embed, precision=lax.Precision.HIGHEST) + atom_features
    masses = jnp.dot(onehot, jnp.array(MASSES, dtype=jnp.float32), precision=lax.Precision.HIGHEST)
    values_start = jnp.dot(h_start, w_value[0].astype(jnp.float32), precision=lax.Precision.HIGHEST)
    lists_all = global_lists(neighbours, ghost_rows)

    def bead_force(bead_pair):
        position, lists = bead_pair

        def energy(xyz):
            extended = xyz[None]
            hidden_zero = h_start[None]
            values_zero = values_start[None]
            hidden_one = mix_layer(hidden_zero, edge_messages(values_zero, extended, lists[None], w_filter[0]), w_out[0])
            values_one = value_rows(hidden_one, w_value[1])
            hidden_two = mix_layer(hidden_one, edge_messages(values_one, extended, lists[None], w_filter[1]), w_out[1])
            return jnp.sum(jax.nn.silu(hidden_two) * readout)
        return -jax.grad(energy)(position)
    forces = lax.map(bead_force, (coords, lists_all))
    state = jnp.concatenate([coords, momenta + 0.5 * STEP_DT * forces], axis=1)
    matrix, omegas = normal_table(BEADS)
    normal_modes = jnp.einsum('jk,jcn->kcn', matrix, state, precision=lax.Precision.HIGHEST)
    normal_modes = advance(normal_modes, omegas, masses)
    result = jnp.einsum('jk,kcn->jcn', matrix, normal_modes, precision=lax.Precision.HIGHEST)
    return (result[:, :3], result[:, 3:])
```

```python
import functools
import math

import jax
import jax.numpy as jnp
from jax import lax
from jax.experimental import pallas as pl
from jax.experimental.pallas import tpu as pltpu
from jax.sharding import PartitionSpec as P

MASSES = (1.008, 12.011, 14.007, 15.999, 30.974)
STEP_DT = 1.0
OMEGA_P = 0.6
WIDTH = 3.125
SPACING = 0.25
SOFTEN = 0.01

MESH = pl.DeviceIdType.MESH
BF16 = jnp.bfloat16
F32 = jnp.float32
GROUP = 4


def dot(a, b):
    return jnp.dot(a, b, preferred_element_type=F32)


def dot_nt(a, b):
    return lax.dot_general(a, b, (((1,), (1,)), ((), ())), preferred_element_type=F32)


def split(x):
    hi = x.astype(BF16)
    return hi, (x - hi.astype(F32)).astype(BF16)


def stacked(x):
    hi, lo = split(x)
    return jnp.concatenate([hi, lo, hi], axis=0)


def ring_tables(count):
    omegas = [2.0 * OMEGA_P * math.sin(math.pi * k / count) for k in range(count)]

    def kernel_of(g):
        return [
            sum(g(w) * math.cos(2.0 * math.pi * k * d / count) for k, w in enumerate(omegas)) / count
            for d in range(count)
        ]

    keep = kernel_of(lambda w: math.cos(w * STEP_DT))
    drift = kernel_of(lambda w: math.sin(w * STEP_DT) / w if w > 0.0 else STEP_DT)
    spring = kernel_of(lambda w: w * math.sin(w * STEP_DT))
    return keep, drift, spring


def kernel(
    n_bead,
    n_space,
    coords,
    momenta,
    species,
    feats,
    nbr,
    ghost_rows,
    embed,
    w_filter,
    w_value,
    w_out,
    readout,
    out_q,
    out_p,
    sel,
    handed,
    pos,
    text,
    halo0_out,
    halo0_in,
    halo1_out,
    halo1_in,
    grad_out,
    grad_in,
    pgrad_out,
    pgrad_in,
    state,
    force,
    offs,
    rads,
    gv,
    p0,
    f1,
    f1d,
    g1,
    msum,
    h0,
    h1,
    u0,
    v1,
    back,
    dh,
    dms,
    drs,
    dv,
    dpos,
    fown,
    halo_send,
    halo_recv,
    state_send,
    state_recv,
    force_send,
    force_recv,
):
    beads, atoms = 2, coords.shape[2]
    ghosts = ghost_rows.shape[1] // 2
    channels = feats.shape[1]
    slots = nbr.shape[1]
    groups = slots // GROUP
    wide = GROUP * atoms
    me_b = lax.axis_index("bead")
    me_s = lax.axis_index("space")
    left = lax.rem(me_s + n_space - 1, n_space)
    right = lax.rem(me_s + 1, n_space)

    barrier = pltpu.get_barrier_semaphore()
    for side in (left, right):
        pl.semaphore_signal(barrier, inc=1, device_id={"space": side}, device_id_type=MESH)
    for o in range(1, n_bead):
        peer = lax.rem(me_b + o, n_bead)
        pl.semaphore_signal(barrier, inc=1, device_id={"bead": peer}, device_id_type=MESH)

    def to_side(number, src, dst_in, going_left):
        mine, theirs = (0, 1) if going_left else (1, 0)
        return pltpu.make_async_remote_copy(
            src_ref=src.at[mine],
            dst_ref=dst_in.at[theirs],
            send_sem=halo_send.at[number, mine],
            recv_sem=halo_recv.at[number, theirs],
            device_id={"space": left if going_left else right},
            device_id_type=MESH,
        )

    def both_sides(number, src, dst_in):
        return [to_side(number, src, dst_in, True), to_side(number, src, dst_in, False)]

    def to_beads(src, buffer, send, recv):
        return [
            pltpu.make_async_remote_copy(
                src_ref=src,
                dst_ref=buffer.at[o],
                send_sem=send.at[o],
                recv_sem=recv.at[o],
                device_id={"bead": lax.rem(me_b + o, n_bead)},
                device_id_type=MESH,
            )
            for o in range(1, n_bead)
        ]

    kinds = species[...]
    start = jnp.transpose(feats[...])
    mass = jnp.zeros((1, atoms), F32)
    for e in range(embed.shape[0]):
        column = jnp.transpose(jnp.broadcast_to(embed[e : e + 1, :], (128, channels)))
        column = jnp.concatenate([column] * (atoms // 128), axis=1)
        start = start + jnp.where(kinds == e, column, 0.0)
        mass = jnp.where(kinds == e, MASSES[e], mass)
    h0[...] = start
    hi, lo = split(start)
    wv0_t = jnp.transpose(w_value[0].astype(F32)).astype(BF16)
    values_zero = (dot(wv0_t, hi) + dot(wv0_t, lo)).astype(BF16)

    pos[...] = jnp.zeros_like(pos)
    for b in range(beads):
        for c in range(3):
            pos[b, c : c + 1, :] = coords[c, b : b + 1, :]
    atom_rows = lax.broadcasted_iota(jnp.int32, (atoms, 2 * ghosts), 0)
    for b in range(beads):
        handed[b] = jnp.where(ghost_rows[b : b + 1, :] == atom_rows, 1.0, 0.0).astype(BF16)
        hi, lo = split(pos[b])
        table = jnp.concatenate([values_zero, hi, lo], axis=0)
        text[b, :, :atoms] = table
        picked = dot(table, handed[b]).astype(BF16)
        halo0_out[0, b] = picked[:, :ghosts]
        halo0_out[1, b] = picked[:, ghosts:]
    state[0, 0:8, :] = pos[0] + pltpu.roll(pos[1], 4, 0)
    state[0, 8:16, :] = jnp.zeros((8, atoms), F32)
    for b in range(beads):
        for c in range(3):
            row = 8 + 4 * b + c
            state[0, row : row + 1, :] = momenta[c, b : b + 1, :]

    pl.semaphore_wait(barrier, 2 + n_bead - 1)
    halo0 = both_sides(0, halo0_out, halo0_in)
    for copy in halo0:
        copy.start()
    state_copies = to_beads(state.at[0], state, state_send, state_recv)
    for copy in state_copies:
        copy.start()

    ext_rows = lax.broadcasted_iota(jnp.int32, (2 * atoms, atoms), 0)

    def select(q, carry):
        b, group = q // groups, lax.rem(q, groups)
        for s in range(GROUP):
            row = nbr[b, pl.ds(group * GROUP + s, 1), :]
            sel[q, :, s * atoms : (s + 1) * atoms] = jnp.where(ext_rows == row, 1.0, 0.0).astype(BF16)
        return carry

    lax.fori_loop(0, beads * groups, select, 0)

    def filter_rows(layer):
        hi, lo = split(jnp.transpose(w_filter[layer]))
        return jnp.concatenate([hi, hi, lo], axis=1)

    def transposed(weight):
        return jnp.transpose(weight.astype(F32)).astype(BF16)

    wf = [filter_rows(0), filter_rows(1)]
    wv1_t = transposed(w_value[1])
    wo_t = [transposed(w_out[0]), transposed(w_out[1])]
    read = jnp.transpose(jnp.broadcast_to(readout[...], (128, channels)))
    read = jnp.concatenate([read] * (atoms // 128), axis=1)
    msum[...] = jnp.zeros_like(msum)
    dv[...] = jnp.zeros_like(dv)
    dpos[...] = jnp.zeros_like(dpos)
    fown[...] = jnp.zeros_like(fown)

    for copy in halo0:
        copy.wait_recv()
    for b in range(beads):
        text[b, :, atoms : atoms + ghosts] = halo0_in[0, b]
        text[b, :, atoms + ghosts :] = halo0_in[1, b]

    centers = SPACING * lax.broadcasted_iota(jnp.int32, (16, atoms), 0).astype(F32)

    def layer_zero(q, carry):
        b = q // groups
        got = dot(text[b], sel[q])
        gv[q] = got[:channels]
        acc = jnp.zeros((channels, atoms), F32)
        for s in range(GROUP):
            here = slice(s * atoms, (s + 1) * atoms)
            off = got[channels : channels + 8, here] + got[channels + 8 :, here] - pos[b]
            offs[q, 0:8, here] = off
            square = jnp.sum(off * off, axis=0, keepdims=True) + SOFTEN
            inverse = lax.rsqrt(square)
            offs[q, 8:16, here] = jnp.broadcast_to(inverse, (8, atoms))
            t = square * inverse - centers
            rad = jnp.exp(-WIDTH * (t * t))
            rads[q, 0, :, here] = stacked(rad)
            rads[q, 1, :, here] = stacked((-2.0 * WIDTH) * (t * rad))
            acc = acc + dot(wf[0], rads[q, 0, :, here]) * gv[q, :, here]
        msum[0, b] += acc
        return carry

    lax.fori_loop(0, beads * groups, layer_zero, 0)

    for b in range(beads):
        update = dot(wo_t[0], msum[0, b].astype(BF16))
        u0[b] = update
        hidden = h0[...] + update * jax.nn.sigmoid(update)
        h1[b] = hidden
        value = dot(wv1_t, hidden.astype(BF16)).astype(BF16)
        v1[b] = value
        picked = dot(value, handed[b]).astype(BF16)
        halo1_out[0, b] = picked[:, :ghosts]
        halo1_out[1, b] = picked[:, ghosts:]
    halo1 = both_sides(1, halo1_out, halo1_in)
    for copy in halo1:
        copy.start()

    def between(q, carry):
        b = q // groups
        g1[q] = dot(v1[b], sel[q, :atoms, :])
        for s in range(GROUP):
            here = slice(s * atoms, (s + 1) * atoms)
            p0[q, :, here] = dot(wf[0], rads[q, 1, :, here]) * gv[q, :, here]
            f1[q, :, here] = dot(wf[1], rads[q, 0, :, here])
            f1d[q, :, here] = dot(wf[1], rads[q, 1, :, here])
        return carry

    lax.fori_loop(0, beads * groups, between, 0)

    for copy in halo1:
        copy.wait_recv()

    def layer_one(q, carry):
        b = q // groups
        far = jnp.concatenate([halo1_in[0, b], halo1_in[1, b]], axis=1)
        got = dot(far, sel[q, atoms:, :])
        acc = jnp.zeros((channels, atoms), F32)
        for s in range(GROUP):
            here = slice(s * atoms, (s + 1) * atoms)
            value = g1[q, :, here] + got[:, here]
            acc = acc + f1[q, :, here] * value
            g1[q, :, here] = f1d[q, :, here] * value
        msum[1, b] += acc
        return carry

    lax.fori_loop(0, beads * groups, layer_one, 0)

    def slope(x, gate):
        return gate * (1.0 + x * (1.0 - gate))

    for b in range(beads):
        update = dot(wo_t[1], msum[1, b].astype(BF16))
        gate = jax.nn.sigmoid(update)
        hidden = h1[b] + update * gate
        grad = read * slope(hidden, jax.nn.sigmoid(hidden))
        dh[b] = grad
        grad = grad * slope(update, gate)
        dms[b] = dot(w_out[1], grad.astype(BF16))

    def ghost_scatter(q, carry):
        b = q // groups
        for s in range(GROUP):
            here = slice(s * atoms, (s + 1) * atoms)
            back[q, :, here] = (f1[q, :, here] * dms[b]).astype(BF16)
        dv[1, b] += dot_nt(back[q], sel[q, atoms:, :])
        return carry

    lax.fori_loop(0, beads * groups, ghost_scatter, 0)
    for b in range(beads):
        value = dv[1, b].astype(BF16)
        grad_out[0, b] = value[:, :ghosts]
        grad_out[1, b] = value[:, ghosts:]
    grads = both_sides(2, grad_out, grad_in)
    for copy in grads:
        copy.start()

    def own_scatter(q, carry):
        b = q // groups
        dv[0, b] += dot_nt(back[q], sel[q, :atoms, :])
        for s in range(GROUP):
            here = slice(s * atoms, (s + 1) * atoms)
            drs[q, :, here] = jnp.sum(dms[b] * g1[q, :, here], axis=0, keepdims=True)
        return carry

    lax.fori_loop(0, beads * groups, own_scatter, 0)

    for copy in grads:
        copy.wait_recv()
    for b in range(beads):
        arrived = jnp.concatenate([grad_in[0, b], grad_in[1, b]], axis=1)
        value = dv[0, b] + dot_nt(arrived, handed[b])
        grad = dh[b] + dot(w_value[1], value.astype(BF16))
        update = u0[b]
        grad = grad * slope(update, jax.nn.sigmoid(update))
        dms[b] = dot(w_out[0], grad.astype(BF16))

    def position_scatter(q, carry):
        b = q // groups
        parts = []
        acc = jnp.zeros((8, atoms), F32)
        for s in range(GROUP):
            here = slice(s * atoms, (s + 1) * atoms)
            slot = drs[q, :, here] + jnp.sum(dms[b] * p0[q, :, here], axis=0, keepdims=True)
            part = offs[q, 0:8, here] * offs[q, 8:16, here] * slot
            acc = acc + part
            parts.append(jnp.concatenate(split(part), axis=0))
        fown[b] += acc
        dpos[b] += dot_nt(jnp.concatenate(parts, axis=1), sel[q])
        return carry

    lax.fori_loop(0, beads * groups, position_scatter, 0)
    for b in range(beads):
        total = dpos[b, 0:8, :] + dpos[b, 8:16, :]
        fown[b] = total[:, :atoms] - fown[b]
        pgrad_out[0, b] = total[:, atoms : atoms + ghosts]
        pgrad_out[1, b] = total[:, atoms + ghosts :]
    pgrads = both_sides(3, pgrad_out, pgrad_in)
    for copy in pgrads:
        copy.start()

    keep, drift, spring = ring_tables(2 * n_bead)
    lower = lax.broadcasted_iota(jnp.int32, (8, atoms), 0) >= 4

    def spread(table, sources):
        same = jnp.zeros((8, atoms), F32)
        other = jnp.zeros((8, atoms), F32)
        count = len(table)
        for o, source in enumerate(sources):
            same = same + table[(2 * o) % count] * source
            other = other + jnp.where(lower, table[(2 * o - 1) % count], table[(2 * o + 1) % count]) * source
        return same + pltpu.roll(other, 4, 0)

    for copy in state_copies:
        copy.wait_recv()
    q_all = [state[o, 0:8, :] for o in range(n_bead)]
    p_all = [state[o, 8:16, :] for o in range(n_bead)]
    q_next = spread(keep, q_all) + spread(drift, p_all) / mass
    p_next = spread(keep, p_all) - mass * spread(spring, q_all)

    for copy in pgrads:
        copy.wait_recv()
    for b in range(beads):
        arrived = jnp.concatenate([pgrad_in[0, b], pgrad_in[1, b]], axis=1)
        placed = dot_nt(jnp.concatenate(split(arrived), axis=0), handed[b])
        fown[b] = (-0.5 * STEP_DT) * (fown[b] + placed[:8] + placed[8:])
    force[0] = fown[0] + pltpu.roll(fown[1], 4, 0)
    force_copies = to_beads(force.at[0], force, force_send, force_recv)
    for copy in force_copies:
        copy.start()
    for copy in force_copies:
        copy.wait_recv()
    kicks = [force[o] for o in range(n_bead)]
    q_next = q_next + spread(drift, kicks) / mass
    p_next = p_next + spread(keep, kicks)
    for b in range(beads):
        for c in range(3):
            row = 4 * b + c
            out_q[c, b : b + 1, :] = q_next[row : row + 1, :]
            out_p[c, b : b + 1, :] = p_next[row : row + 1, :]
    for copy in halo0 + halo1 + grads + pgrads + state_copies + force_copies:
        copy.wait_send()


def local(
    coords,
    momenta,
    species,
    atom_features,
    neighbours,
    ghost_rows,
    embed,
    w_filter,
    w_value,
    w_out,
    readout,
):
    n_bead, n_space = lax.axis_size("bead"), lax.axis_size("space")
    beads, _, atoms = coords.shape
    slots = neighbours.shape[2]
    ghosts = ghost_rows.shape[1] // 2
    channels = embed.shape[1]
    steps = beads * slots // GROUP
    wide = GROUP * atoms
    rows = channels + 16
    vmem = pl.BlockSpec(memory_space=pltpu.VMEM)
    big = pltpu.VMEM((steps, channels, wide), F32)
    per_bead = pltpu.VMEM((beads, channels, atoms), F32)
    shape = jax.ShapeDtypeStruct((3, beads, atoms), F32)
    q_next, p_next = pl.pallas_call(
        functools.partial(kernel, n_bead, n_space),
        out_shape=(shape, shape),
        in_specs=[vmem] * 11,
        out_specs=(vmem, vmem),
        scratch_shapes=[
            pltpu.VMEM((steps, 2 * atoms, wide), BF16),
            pltpu.VMEM((beads, atoms, 2 * ghosts), BF16),
            pltpu.VMEM((beads, 8, atoms), F32),
            pltpu.VMEM((beads, rows, 2 * atoms), BF16),
            pltpu.VMEM((2, beads, rows, ghosts), BF16),
            pltpu.VMEM((2, beads, rows, ghosts), BF16),
            pltpu.VMEM((2, beads, channels, ghosts), BF16),
            pltpu.VMEM((2, beads, channels, ghosts), BF16),
            pltpu.VMEM((2, beads, channels, ghosts), BF16),
            pltpu.VMEM((2, beads, channels, ghosts), BF16),
            pltpu.VMEM((2, beads, 8, ghosts), F32),
            pltpu.VMEM((2, beads, 8, ghosts), F32),
            pltpu.VMEM((n_bead, 16, atoms), F32),
            pltpu.VMEM((n_bead, 8, atoms), F32),
            pltpu.VMEM((steps, 16, wide), F32),
            pltpu.VMEM((steps, 2, 48, wide), BF16),
            big,
            big,
            big,
            big,
            big,
            pltpu.VMEM((2, beads, channels, atoms), F32),
            pltpu.VMEM((channels, atoms), F32),
            per_bead,
            per_bead,
            pltpu.VMEM((beads, channels, atoms), BF16),
            pltpu.VMEM((steps, channels, wide), BF16),
            per_bead,
            per_bead,
            pltpu.VMEM((steps, 1, wide), F32),
            pltpu.VMEM((2, beads, channels, atoms), F32),
            pltpu.VMEM((beads, 16, 2 * atoms), F32),
            pltpu.VMEM((beads, 8, atoms), F32),
            pltpu.SemaphoreType.DMA((4, 2)),
            pltpu.SemaphoreType.DMA((4, 2)),
            pltpu.SemaphoreType.DMA((n_bead,)),
            pltpu.SemaphoreType.DMA((n_bead,)),
            pltpu.SemaphoreType.DMA((n_bead,)),
            pltpu.SemaphoreType.DMA((n_bead,)),
        ],
        compiler_params=pltpu.CompilerParams(
            collective_id=0, has_side_effects=True, vmem_limit_bytes=58 * 1024 * 1024
        ),
    )(
        jnp.transpose(coords, (1, 0, 2)),
        jnp.transpose(momenta, (1, 0, 2)),
        species.reshape(1, atoms),
        atom_features,
        jnp.transpose(neighbours, (0, 2, 1)),
        ghost_rows,
        embed,
        w_filter,
        w_value,
        w_out,
        readout.reshape(1, channels),
    )
    return jnp.transpose(q_next, (1, 0, 2)), jnp.transpose(p_next, (1, 0, 2))


def solution(mesh):
    placed = (
        P("bead", None, "space"),
        P("bead", None, "space"),
        P("space"),
        P("space", None),
        P("bead", "space", None),
        P("bead", "space"),
        P(),
        P(),
        P(),
        P(),
        P(),
    )
    return jax.shard_map(
        local,
        mesh=mesh,
        in_specs=placed,
        out_specs=(P("bead", None, "space"), P("bead", None, "space")),
        check_vma=False,
    )
```

```python
import functools
import math

import jax
import jax.numpy as jnp
from jax import lax
from jax.experimental import pallas as pl
from jax.experimental.pallas import tpu as pltpu
from jax.sharding import PartitionSpec as P

MASSES = (1.008, 12.011, 14.007, 15.999, 30.974)
STEP_DT = 1.0
OMEGA_P = 0.6
WIDTH = 3.125
SPACING = 0.25
SOFTEN = 0.01

MESH = pl.DeviceIdType.MESH
BF16 = jnp.bfloat16
F32 = jnp.float32
GROUP = 4


def dot(a, b):
    return jnp.dot(a, b, preferred_element_type=F32)


def dot_nt(a, b):
    return lax.dot_general(a, b, (((1,), (1,)), ((), ())), preferred_element_type=F32)


def split(x):
    hi = x.astype(BF16)
    return hi, (x - hi.astype(F32)).astype(BF16)


def stacked(x):
    hi, lo = split(x)
    return jnp.concatenate([hi, lo, hi], axis=0)


def ring_tables(count):
    omegas = [2.0 * OMEGA_P * math.sin(math.pi * k / count) for k in range(count)]

    def kernel_of(g):
        return [
            sum(g(w) * math.cos(2.0 * math.pi * k * d / count) for k, w in enumerate(omegas)) / count
            for d in range(count)
        ]

    keep = kernel_of(lambda w: math.cos(w * STEP_DT))
    drift = kernel_of(lambda w: math.sin(w * STEP_DT) / w if w > 0.0 else STEP_DT)
    spring = kernel_of(lambda w: w * math.sin(w * STEP_DT))
    return keep, drift, spring


def kernel(
    n_bead,
    n_space,
    coords,
    momenta,
    species,
    feats,
    nbr,
    ghost_rows,
    embed,
    w_filter,
    w_value,
    w_out,
    readout,
    out_q,
    out_p,
    sel,
    handed,
    pos,
    text,
    halo0_out,
    halo0_in,
    halo1_out,
    halo1_in,
    grad_out,
    grad_in,
    pgrad_out,
    pgrad_in,
    state,
    force,
    offs,
    rads,
    gv,
    p0,
    f1,
    f1d,
    g1,
    h0,
    h1,
    u0,
    v1,
    back,
    parts,
    dh,
    dms,
    drs,
    dv,
    fown,
    halo_send,
    halo_recv,
    state_send,
    state_recv,
    force_send,
    force_recv,
):
    beads, atoms = 2, coords.shape[2]
    ghosts = ghost_rows.shape[1] // 2
    channels = feats.shape[1]
    slots = nbr.shape[1]
    groups = slots // GROUP
    wide = GROUP * atoms
    me_b = lax.axis_index("bead")
    me_s = lax.axis_index("space")
    left = lax.rem(me_s + n_space - 1, n_space)
    right = lax.rem(me_s + 1, n_space)

    barrier = pltpu.get_barrier_semaphore()
    for side in (left, right):
        pl.semaphore_signal(barrier, inc=1, device_id={"space": side}, device_id_type=MESH)
    for o in range(1, n_bead):
        peer = lax.rem(me_b + o, n_bead)
        pl.semaphore_signal(barrier, inc=1, device_id={"bead": peer}, device_id_type=MESH)

    def both_sides(number, b, src, dst):
        return [
            pltpu.make_async_remote_copy(
                src_ref=src.at[b, mine],
                dst_ref=dst.at[b, 1 - mine],
                send_sem=halo_send.at[number, b, mine],
                recv_sem=halo_recv.at[number, b, 1 - mine],
                device_id={"space": side},
                device_id_type=MESH,
            )
            for mine, side in enumerate((left, right))
        ]

    def to_beads(buffer, part, send, recv):
        return [
            pltpu.make_async_remote_copy(
                src_ref=part(buffer, 0),
                dst_ref=part(buffer, o),
                send_sem=send.at[o],
                recv_sem=recv.at[o],
                device_id={"bead": lax.rem(me_b + o, n_bead)},
                device_id_type=MESH,
            )
            for o in range(1, n_bead)
        ]

    def start_all(copies):
        for copy in copies:
            copy.start()

    def arrive(copies):
        for copy in copies:
            copy.wait_recv()

    kinds = species[...]
    start = jnp.transpose(feats[...])
    mass = jnp.zeros((1, atoms), F32)
    for e in range(embed.shape[0]):
        column = jnp.transpose(jnp.broadcast_to(embed[e : e + 1, :], (128, channels)))
        column = jnp.concatenate([column] * (atoms // 128), axis=1)
        start = start + jnp.where(kinds == e, column, 0.0)
        mass = jnp.where(kinds == e, MASSES[e], mass)
    h0[...] = start
    hi, lo = split(start)
    wv0_t = jnp.transpose(w_value[0].astype(F32)).astype(BF16)
    values_zero = (dot(wv0_t, hi) + dot(wv0_t, lo)).astype(BF16)

    pos[...] = jnp.zeros_like(pos)
    for b in range(beads):
        for c in range(3):
            pos[b, c : c + 1, :] = coords[c, b : b + 1, :]
    atom_rows = lax.broadcasted_iota(jnp.int32, (atoms, 2 * ghosts), 0)
    for b in range(beads):
        handed[b] = jnp.where(ghost_rows[b : b + 1, :] == atom_rows, 1.0, 0.0).astype(BF16)
        hi, lo = split(pos[b])
        table = jnp.concatenate([values_zero, hi, lo], axis=0)
        text[b, :, :atoms] = table
        picked = dot(table, handed[b]).astype(BF16)
        halo0_out[b, 0] = picked[:, :ghosts]
        halo0_out[b, 1] = picked[:, ghosts:]

    pl.semaphore_wait(barrier, 2 + n_bead - 1)
    halo0 = [both_sides(0, b, halo0_out, halo0_in) for b in range(beads)]
    start_all(halo0[0])
    start_all(halo0[1])

    ext_rows = lax.broadcasted_iota(jnp.int32, (2 * atoms, atoms), 0)
    for b in range(beads):
        for s in range(slots):
            row = nbr[b, s : s + 1, :]
            sel[b, :, s * atoms : (s + 1) * atoms] = jnp.where(ext_rows == row, 1.0, 0.0).astype(BF16)

    def filter_rows(layer):
        hi, lo = split(jnp.transpose(w_filter[layer]))
        return jnp.concatenate([hi, hi, lo], axis=1)

    def transposed(weight):
        return jnp.transpose(weight.astype(F32)).astype(BF16)

    wf = [filter_rows(0), filter_rows(1)]
    wv1_t = transposed(w_value[1])
    wo_t = [transposed(w_out[0]), transposed(w_out[1])]
    read = jnp.transpose(jnp.broadcast_to(readout[...], (128, channels)))
    read = jnp.concatenate([read] * (atoms // 128), axis=1)
    state[0] = jnp.zeros(state.shape[1:], F32)
    for b in range(beads):
        for c in range(3):
            state[0, 0, b, c : c + 1, :] = coords[c, b : b + 1, :]
            state[0, 1, b, c : c + 1, :] = momenta[c, b : b + 1, :]

    centers = SPACING * lax.broadcasted_iota(jnp.int32, (16, atoms), 0).astype(F32)
    lanes = [slice(s * atoms, (s + 1) * atoms) for s in range(slots)]
    chunks = [slice(g * wide, (g + 1) * wide) for g in range(groups)]

    def slope(x, gate):
        return gate * (1.0 + x * (1.0 - gate))

    def layer_zero(b):
        text[b, :, atoms : atoms + ghosts] = halo0_in[b, 0]
        text[b, :, atoms + ghosts :] = halo0_in[b, 1]
        acc = jnp.zeros((channels, atoms), F32)
        for g in range(groups):
            got = dot(text[b], sel[b, :, chunks[g]])
            gv[b, :, chunks[g]] = got[:channels]
            for s in range(GROUP):
                here, there = lanes[g * GROUP + s], lanes[s]
                off = got[channels : channels + 8, there] + got[channels + 8 :, there] - pos[b]
                offs[b, 0:8, here] = off
                square = jnp.sum(off * off, axis=0, keepdims=True) + SOFTEN
                inverse = lax.rsqrt(square)
                offs[b, 8:16, here] = jnp.broadcast_to(inverse, (8, atoms))
                t = square * inverse - centers
                rad = jnp.exp(-WIDTH * (t * t))
                rads[b, 0, :, here] = stacked(rad)
                rads[b, 1, :, here] = stacked((-2.0 * WIDTH) * (t * rad))
                acc = acc + dot(wf[0], rads[b, 0, :, here]) * gv[b, :, here]
        update = dot(wo_t[0], acc.astype(BF16))
        u0[b] = update
        hidden = h0[...] + update * jax.nn.sigmoid(update)
        h1[b] = hidden
        value = dot(wv1_t, hidden.astype(BF16)).astype(BF16)
        v1[b] = value
        picked = dot(value, handed[b]).astype(BF16)
        halo1_out[b, 0] = picked[:, :ghosts]
        halo1_out[b, 1] = picked[:, ghosts:]
        copies = both_sides(1, b, halo1_out, halo1_in)
        start_all(copies)
        return copies

    def between(b):
        for g in range(groups):
            g1[b, :, chunks[g]] = dot(v1[b], sel[b, :atoms, chunks[g]])
        for here in lanes:
            p0[b, :, here] = dot(wf[0], rads[b, 1, :, here]) * gv[b, :, here]
            f1[b, :, here] = dot(wf[1], rads[b, 0, :, here])
            f1d[b, :, here] = dot(wf[1], rads[b, 1, :, here])

    def layer_one(b):
        far = jnp.concatenate([halo1_in[b, 0], halo1_in[b, 1]], axis=1)
        acc = jnp.zeros((channels, atoms), F32)
        for g in range(groups):
            got = dot(far, sel[b, atoms:, chunks[g]])
            for s in range(GROUP):
                here, there = lanes[g * GROUP + s], lanes[s]
                value = g1[b, :, here] + got[:, there]
                acc = acc + f1[b, :, here] * value
                g1[b, :, here] = f1d[b, :, here] * value
        update = dot(wo_t[1], acc.astype(BF16))
        gate = jax.nn.sigmoid(update)
        hidden = h1[b] + update * gate
        grad = read * slope(hidden, jax.nn.sigmoid(hidden))
        dh[b] = grad
        grad = grad * slope(update, gate)
        dms[b] = dot(w_out[1], grad.astype(BF16))
        total = jnp.zeros((channels, 2 * ghosts), F32)
        for g in range(groups):
            for s in range(GROUP):
                here = lanes[g * GROUP + s]
                back[b, :, here] = (f1[b, :, here] * dms[b]).astype(BF16)
            total = total + dot_nt(back[b, :, chunks[g]], sel[b, atoms:, chunks[g]])
        value = total.astype(BF16)
        grad_out[b, 0] = value[:, :ghosts]
        grad_out[b, 1] = value[:, ghosts:]
        copies = both_sides(2, b, grad_out, grad_in)
        start_all(copies)
        return copies

    def own_scatter(b):
        total = jnp.zeros((channels, atoms), F32)
        for g in range(groups):
            total = total + dot_nt(back[b, :, chunks[g]], sel[b, :atoms, chunks[g]])
        dv[b] = total
        for here in lanes:
            drs[b, :, here] = jnp.sum(dms[b] * g1[b, :, here], axis=0, keepdims=True)

    def backward(b):
        arrived = jnp.concatenate([grad_in[b, 0], grad_in[b, 1]], axis=1)
        value = dv[b] + dot_nt(arrived, handed[b])
        grad = dh[b] + dot(w_value[1], value.astype(BF16))
        update = u0[b]
        grad = grad * slope(update, jax.nn.sigmoid(update))
        message = dot(w_out[0], grad.astype(BF16))
        acc = jnp.zeros((8, atoms), F32)
        total = jnp.zeros((16, 2 * ghosts), F32)
        for g in range(groups):
            for s in range(GROUP):
                here = lanes[g * GROUP + s]
                slot = drs[b, :, here] + jnp.sum(message * p0[b, :, here], axis=0, keepdims=True)
                part = offs[b, 0:8, here] * offs[b, 8:16, here] * slot
                acc = acc + part
                parts[b, :, here] = jnp.concatenate(split(part), axis=0)
            total = total + dot_nt(parts[b, :, chunks[g]], sel[b, atoms:, chunks[g]])
        total = total[0:8] + total[8:16]
        pgrad_out[b, 0] = total[:, :ghosts]
        pgrad_out[b, 1] = total[:, ghosts:]
        copies = both_sides(3, b, pgrad_out, pgrad_in)
        start_all(copies)
        total = jnp.zeros((16, atoms), F32)
        for g in range(groups):
            total = total + dot_nt(parts[b, :, chunks[g]], sel[b, :atoms, chunks[g]])
        fown[b] = total[0:8] + total[8:16] - acc
        return copies

    def kick(b):
        arrived = jnp.concatenate([pgrad_in[b, 0], pgrad_in[b, 1]], axis=1)
        placed = dot_nt(jnp.concatenate(split(arrived), axis=0), handed[b])
        force[0, b] = ((-0.5 * STEP_DT) * (fown[b] + placed[0:8] + placed[8:16]))[0:4]
        copies = to_beads(force, lambda ref, o: ref.at[o, b], force_send.at[b], force_recv.at[b])
        start_all(copies)
        return copies

    arrive(halo0[0])
    halo1_0 = layer_zero(0)
    arrive(halo0[1])
    states = to_beads(state, lambda ref, o: ref.at[o], state_send, state_recv)
    start_all(states)
    halo1_1 = layer_zero(1)
    between(0)
    arrive(halo1_0)
    grads_0 = layer_one(0)
    between(1)
    arrive(halo1_1)
    grads_1 = layer_one(1)
    own_scatter(0)
    arrive(grads_0)
    pgrads_0 = backward(0)
    own_scatter(1)
    arrive(pgrads_0)
    forces_0 = kick(0)
    arrive(grads_1)
    pgrads_1 = backward(1)

    keep, drift, spring = ring_tables(beads * n_bead)

    def spread(table, sources):
        result = []
        for b in range(beads):
            total = jnp.zeros((4, atoms), F32)
            for o, pair in enumerate(sources):
                for c, source in enumerate(pair):
                    total = total + table[(beads * o + b - c) % len(table)] * source
            result.append(total)
        return result

    arrive(states)
    q_all = [[state[o, 0, c] for c in range(beads)] for o in range(n_bead)]
    p_all = [[state[o, 1, c] for c in range(beads)] for o in range(n_bead)]
    q_next = [x + y / mass for x, y in zip(spread(keep, q_all), spread(drift, p_all))]
    p_next = [x - mass * y for x, y in zip(spread(keep, p_all), spread(spring, q_all))]

    arrive(pgrads_1)
    forces_1 = kick(1)
    arrive(forces_0)
    arrive(forces_1)
    kicks = [[force[o, c] for c in range(beads)] for o in range(n_bead)]
    q_next = [x + y / mass for x, y in zip(q_next, spread(drift, kicks))]
    p_next = [x + y for x, y in zip(p_next, spread(keep, kicks))]
    for b in range(beads):
        for c in range(3):
            out_q[c, b : b + 1, :] = q_next[b][c : c + 1, :]
            out_p[c, b : b + 1, :] = p_next[b][c : c + 1, :]
    for copies in halo0 + [halo1_0, halo1_1, grads_0, grads_1, pgrads_0, pgrads_1, states, forces_0, forces_1]:
        for copy in copies:
            copy.wait_send()


def local(
    coords,
    momenta,
    species,
    atom_features,
    neighbours,
    ghost_rows,
    embed,
    w_filter,
    w_value,
    w_out,
    readout,
):
    n_bead, n_space = lax.axis_size("bead"), lax.axis_size("space")
    beads, _, atoms = coords.shape
    slots = neighbours.shape[2]
    ghosts = ghost_rows.shape[1] // 2
    channels = embed.shape[1]
    edges = slots * atoms
    rows = channels + 16
    vmem = pl.BlockSpec(memory_space=pltpu.VMEM)
    big = pltpu.VMEM((beads, channels, edges), F32)
    per_bead = pltpu.VMEM((beads, channels, atoms), F32)
    shape = jax.ShapeDtypeStruct((3, beads, atoms), F32)
    q_next, p_next = pl.pallas_call(
        functools.partial(kernel, n_bead, n_space),
        out_shape=(shape, shape),
        in_specs=[vmem] * 11,
        out_specs=(vmem, vmem),
        scratch_shapes=[
            pltpu.VMEM((beads, 2 * atoms, edges), BF16),
            pltpu.VMEM((beads, atoms, 2 * ghosts), BF16),
            pltpu.VMEM((beads, 8, atoms), F32),
            pltpu.VMEM((beads, rows, 2 * atoms), BF16),
            pltpu.VMEM((beads, 2, rows, ghosts), BF16),
            pltpu.VMEM((beads, 2, rows, ghosts), BF16),
            pltpu.VMEM((beads, 2, channels, ghosts), BF16),
            pltpu.VMEM((beads, 2, channels, ghosts), BF16),
            pltpu.VMEM((beads, 2, channels, ghosts), BF16),
            pltpu.VMEM((beads, 2, channels, ghosts), BF16),
            pltpu.VMEM((beads, 2, 8, ghosts), F32),
            pltpu.VMEM((beads, 2, 8, ghosts), F32),
            pltpu.VMEM((n_bead, 2, beads, 4, atoms), F32),
            pltpu.VMEM((n_bead, beads, 4, atoms), F32),
            pltpu.VMEM((beads, 16, edges), F32),
            pltpu.VMEM((beads, 2, 48, edges), BF16),
            big,
            big,
            big,
            big,
            big,
            pltpu.VMEM((channels, atoms), F32),
            per_bead,
            per_bead,
            pltpu.VMEM((beads, channels, atoms), BF16),
            pltpu.VMEM((beads, channels, edges), BF16),
            pltpu.VMEM((beads, 16, edges), BF16),
            per_bead,
            per_bead,
            pltpu.VMEM((beads, 1, edges), F32),
            per_bead,
            pltpu.VMEM((beads, 8, atoms), F32),
            pltpu.SemaphoreType.DMA((4, beads, 2)),
            pltpu.SemaphoreType.DMA((4, beads, 2)),
            pltpu.SemaphoreType.DMA((n_bead,)),
            pltpu.SemaphoreType.DMA((n_bead,)),
            pltpu.SemaphoreType.DMA((beads, n_bead)),
            pltpu.SemaphoreType.DMA((beads, n_bead)),
        ],
        compiler_params=pltpu.CompilerParams(
            collective_id=0, has_side_effects=True, vmem_limit_bytes=58 * 1024 * 1024
        ),
    )(
        jnp.transpose(coords, (1, 0, 2)),
        jnp.transpose(momenta, (1, 0, 2)),
        species.reshape(1, atoms),
        atom_features,
        jnp.transpose(neighbours, (0, 2, 1)),
        ghost_rows,
        embed,
        w_filter,
        w_value,
        w_out,
        readout.reshape(1, channels),
    )
    return jnp.transpose(q_next, (1, 0, 2)), jnp.transpose(p_next, (1, 0, 2))


def solution(mesh):
    placed = (
        P("bead", None, "space"),
        P("bead", None, "space"),
        P("space"),
        P("space", None),
        P("bead", "space", None),
        P("bead", "space"),
        P(),
        P(),
        P(),
        P(),
        P(),
    )
    return jax.shard_map(
        local,
        mesh=mesh,
        in_specs=placed,
        out_specs=(P("bead", None, "space"), P("bead", None, "space")),
        check_vma=False,
    )
```

```python
import functools
import math

import jax
import jax.numpy as jnp
from jax import lax
from jax.experimental import pallas as pl
from jax.experimental.pallas import tpu as pltpu
from jax.sharding import PartitionSpec as P

MASSES = (1.008, 12.011, 14.007, 15.999, 30.974)
STEP_DT = 1.0
OMEGA_P = 0.6
WIDTH = 3.125
SPACING = 0.25
SOFTEN = 0.01

MESH = pl.DeviceIdType.MESH
BF16 = jnp.bfloat16
F32 = jnp.float32
GROUP = 4


def dot(a, b):
    return jnp.dot(a, b, preferred_element_type=F32)


def one_hot(index, places):
    index = jnp.broadcast_to(index, places.shape)
    return jnp.where(index == places, jnp.ones(places.shape, BF16), jnp.zeros(places.shape, BF16))


def split(x):
    hi = x.astype(BF16)
    return hi, (x - hi.astype(F32)).astype(BF16)


def stacked(x):
    hi, lo = split(x)
    return jnp.concatenate([hi, lo, hi], axis=0)


def ring_tables(count):
    omegas = [2.0 * OMEGA_P * math.sin(math.pi * k / count) for k in range(count)]

    def kernel_of(g):
        return [
            sum(g(w) * math.cos(2.0 * math.pi * k * d / count) for k, w in enumerate(omegas)) / count
            for d in range(count)
        ]

    keep = kernel_of(lambda w: math.cos(w * STEP_DT))
    drift = kernel_of(lambda w: math.sin(w * STEP_DT) / w if w > 0.0 else STEP_DT)
    spring = kernel_of(lambda w: w * math.sin(w * STEP_DT))
    return keep, drift, spring


def kernel(
    n_bead,
    n_space,
    coords,
    momenta,
    species,
    feats,
    nbr,
    ghost_rows,
    embed,
    w_filter,
    w_value,
    w_out,
    readout,
    out_q,
    out_p,
    sel,
    sel_t,
    handed,
    given,
    pos,
    text,
    halo0_out,
    halo0_in,
    halo1_out,
    halo1_in,
    grad_out,
    grad_in,
    pgrad_out,
    pgrad_in,
    state,
    kicked,
    momentum,
    offs,
    rads,
    gv,
    p0,
    f1,
    g1,
    h0,
    h1,
    u0,
    v1,
    back,
    parts,
    dh,
    dms,
    drs,
    dv,
    fown,
    halo_send,
    halo_recv,
    state_send,
    state_recv,
    kick_send,
    kick_recv,
    ready,
):
    beads, atoms = 2, coords.shape[2]
    ghosts = ghost_rows.shape[1] // 2
    channels = feats.shape[1]
    slots = nbr.shape[1]
    groups = slots // GROUP
    wide = GROUP * atoms
    me_b = lax.axis_index("bead")
    me_s = lax.axis_index("space")
    left = lax.rem(me_s + n_space - 1, n_space)
    right = lax.rem(me_s + 1, n_space)

    def signal(semaphore, offsets):
        for o in offsets:
            peer = lax.rem(me_b + (o % n_bead), n_bead)
            pl.semaphore_signal(semaphore, inc=1, device_id={"bead": peer}, device_id_type=MESH)

    near, far_out = (1, -1, 8), (2, -2, 8)
    barrier = pltpu.get_barrier_semaphore()
    for side in (left, right):
        pl.semaphore_signal(barrier, inc=1, device_id={"space": side}, device_id_type=MESH)
    signal(barrier, near)

    halos = ((halo0_out, halo0_in), (halo1_out, halo1_in), (grad_out, grad_in), (pgrad_out, pgrad_in))

    def halo(number, b):
        src, dst = halos[number]
        return [
            pltpu.make_async_remote_copy(
                src_ref=src.at[b, mine],
                dst_ref=dst.at[b, 1 - mine],
                send_sem=halo_send.at[number, b, mine],
                recv_sem=halo_recv.at[number, b, 1 - mine],
                device_id={"space": side},
                device_id_type=MESH,
            )
            for mine, side in enumerate((left, right))
        ]

    def to_beads(source, part, send, recv):
        return [
            pltpu.make_async_remote_copy(
                src_ref=source,
                dst_ref=part(o),
                send_sem=send.at[o],
                recv_sem=recv.at[o],
                device_id={"bead": lax.rem(me_b + o, n_bead)},
                device_id_type=MESH,
            )
            for o in range(1, n_bead)
        ]

    def states():
        return to_beads(coords, lambda o: state.at[o], state_send, state_recv)

    def kicks(b):
        return to_beads(kicked.at[0, b], lambda o: kicked.at[o, b], kick_send.at[b], kick_recv.at[b])

    def start_all(copies):
        for copy in copies:
            copy.start()

    def arrive(copies):
        for copy in copies:
            copy.wait_recv()

    kinds = species[...]
    start = jnp.transpose(feats[...])
    mass = jnp.zeros((1, atoms), F32)
    for e in range(embed.shape[0]):
        column = jnp.transpose(jnp.broadcast_to(embed[e : e + 1, :], (128, channels)))
        column = jnp.concatenate([column] * (atoms // 128), axis=1)
        start = start + jnp.where(kinds == e, column, 0.0)
        mass = jnp.where(kinds == e, MASSES[e], mass)
    h0[...] = start
    hi, lo = split(start)
    wv0_t = jnp.transpose(w_value[0].astype(F32)).astype(BF16)
    values_zero = (dot(wv0_t, hi) + dot(wv0_t, lo)).astype(BF16)

    pos[...] = jnp.zeros_like(pos)
    for b in range(beads):
        for c in range(3):
            pos[b, c : c + 1, :] = coords[c, b : b + 1, :]
    atom_rows = lax.broadcasted_iota(jnp.int32, (atoms, atoms), 0).astype(F32).astype(BF16)
    atom_lanes = lax.broadcasted_iota(jnp.int32, (atoms, atoms), 1).astype(F32).astype(BF16)
    for b in range(beads):
        handed[b] = one_hot(ghost_rows[b : b + 1, :].astype(F32).astype(BF16), atom_rows)
        hi, lo = split(pos[b])
        table = jnp.concatenate([values_zero, hi, lo], axis=0)
        text[b] = table
        picked = dot(table, handed[b]).astype(BF16)
        halo0_out[b, 0] = picked[:, :ghosts]
        halo0_out[b, 1] = picked[:, ghosts:]

    pl.semaphore_wait(barrier, 2 + len(near))
    for b in range(beads):
        start_all(halo(0, b))
    signal(ready.at[0], near)

    for b in range(beads):
        lists = nbr[b].astype(F32)
        halves = [lists.astype(BF16), (lists - float(atoms)).astype(BF16)]
        for s in range(slots):
            here = slice(s * atoms, (s + 1) * atoms)
            for half, value in enumerate(halves):
                sel[b, half * atoms : (half + 1) * atoms, here] = one_hot(value[s : s + 1, :], atom_rows)
        got = dot(text[b], sel[b, :atoms, :])
        gv[b] = got[:channels]
        offs[b] = got[channels:]
    for b in range(beads):
        marks = jnp.broadcast_to(ghost_rows[b : b + 1, :], (8, 2 * ghosts))
        columns = jnp.transpose(jnp.concatenate([nbr[b], marks], axis=0)).astype(F32)
        given[b] = one_hot(columns[:, slots : slots + 1].astype(BF16), atom_lanes)
        for s in range(slots):
            here = slice(s * atoms, (s + 1) * atoms)
            column = jnp.broadcast_to(columns[:, s : s + 1], (atoms, atoms))
            sel_t[b, here, :atoms] = one_hot(column.astype(BF16), atom_lanes)
            sel_t[b, here, atoms:] = one_hot((column - float(atoms)).astype(BF16), atom_lanes)

    def filter_rows(layer):
        hi, lo = split(jnp.transpose(w_filter[layer]))
        return jnp.concatenate([hi, hi, lo], axis=1)

    def transposed(weight):
        return jnp.transpose(weight.astype(F32)).astype(BF16)

    wf = [filter_rows(0), filter_rows(1)]
    wv1_t = transposed(w_value[1])
    wo_t = [transposed(w_out[0]), transposed(w_out[1])]
    read = jnp.transpose(jnp.broadcast_to(readout[...], (128, channels)))
    read = jnp.concatenate([read] * (atoms // 128), axis=1)
    momentum[...] = jnp.zeros_like(momentum)
    for b in range(beads):
        for c in range(3):
            momentum[b, c : c + 1, :] = momenta[c, b : b + 1, :]

    centers = SPACING * lax.broadcasted_iota(jnp.int32, (16, atoms), 0).astype(F32)
    lanes = [slice(s * atoms, (s + 1) * atoms) for s in range(slots)]
    chunks = [slice(g * wide, (g + 1) * wide) for g in range(groups)]

    def slope(x, gate):
        return gate * (1.0 + x * (1.0 - gate))

    def layer_zero(b):
        far = jnp.concatenate([halo0_in[b, 0], halo0_in[b, 1]], axis=1)
        acc = jnp.zeros((channels, atoms), F32)
        for g in range(groups):
            got = dot(far, sel[b, atoms:, chunks[g]])
            for s in range(GROUP):
                here, there = lanes[g * GROUP + s], lanes[s]
                place = got[channels:, there] + offs[b, :, here]
                off = place[0:8] + place[8:16] - pos[b]
                offs[b, 0:8, here] = off
                square = jnp.sum(off * off, axis=0, keepdims=True) + SOFTEN
                inverse = lax.rsqrt(square)
                offs[b, 8:16, here] = jnp.broadcast_to(inverse, (8, atoms))
                t = square * inverse - centers
                rad = jnp.exp(-WIDTH * (t * t))
                rads[b, 0, :, here] = stacked(rad)
                rads[b, 1, :, here] = stacked((-2.0 * WIDTH) * (t * rad))
                value = got[:channels, there] + gv[b, :, here]
                gv[b, :, here] = value
                acc = acc + dot(wf[0], rads[b, 0, :, here]) * value
        update = dot(wo_t[0], acc.astype(BF16))
        u0[b] = update
        hidden = h0[...] + update * jax.nn.sigmoid(update)
        h1[b] = hidden
        value = dot(wv1_t, hidden.astype(BF16)).astype(BF16)
        v1[b] = value
        picked = dot(value, handed[b]).astype(BF16)
        halo1_out[b, 0] = picked[:, :ghosts]
        halo1_out[b, 1] = picked[:, ghosts:]
        start_all(halo(1, b))

    def between(b):
        for g in range(groups):
            g1[b, :, chunks[g]] = dot(v1[b], sel[b, :atoms, chunks[g]])
        for here in lanes:
            f1[b, :, here] = dot(wf[1], rads[b, 0, :, here])

    def layer_one(b):
        far = jnp.concatenate([halo1_in[b, 0], halo1_in[b, 1]], axis=1)
        acc = jnp.zeros((channels, atoms), F32)
        for g in range(groups):
            got = dot(far, sel[b, atoms:, chunks[g]])
            for s in range(GROUP):
                here, there = lanes[g * GROUP + s], lanes[s]
                value = g1[b, :, here] + got[:, there]
                acc = acc + f1[b, :, here] * value
                g1[b, :, here] = value
        update = dot(wo_t[1], acc.astype(BF16))
        gate = jax.nn.sigmoid(update)
        hidden = h1[b] + update * gate
        grad = read * slope(hidden, jax.nn.sigmoid(hidden))
        dh[b] = grad
        grad = grad * slope(update, gate)
        dms[b] = dot(w_out[1], grad.astype(BF16))
        total = jnp.zeros((channels, 2 * ghosts), F32)
        for g in range(groups):
            for s in range(GROUP):
                here = lanes[g * GROUP + s]
                back[b, :, here] = (f1[b, :, here] * dms[b]).astype(BF16)
            total = total + dot(back[b, :, chunks[g]], sel_t[b, chunks[g], atoms:])
        value = total.astype(BF16)
        grad_out[b, 0] = value[:, :ghosts]
        grad_out[b, 1] = value[:, ghosts:]
        start_all(halo(2, b))

    def own_scatter(b):
        total = jnp.zeros((channels, atoms), F32)
        for g in range(groups):
            total = total + dot(back[b, :, chunks[g]], sel_t[b, chunks[g], :atoms])
        dv[b] = total
        for here in lanes:
            p0[b, :, here] = dot(wf[0], rads[b, 1, :, here]) * gv[b, :, here]
            change = dot(wf[1], rads[b, 1, :, here]) * g1[b, :, here]
            drs[b, :, here] = jnp.sum(dms[b] * change, axis=0, keepdims=True)

    def backward(b):
        arrived = jnp.concatenate([grad_in[b, 0], grad_in[b, 1]], axis=1)
        value = dv[b] + dot(arrived, given[b])
        grad = dh[b] + dot(w_value[1], value.astype(BF16))
        update = u0[b]
        grad = grad * slope(update, jax.nn.sigmoid(update))
        message = dot(w_out[0], grad.astype(BF16))
        acc = jnp.zeros((8, atoms), F32)
        total = jnp.zeros((16, 2 * ghosts), F32)
        for g in range(groups):
            for s in range(GROUP):
                here = lanes[g * GROUP + s]
                slot = drs[b, :, here] + jnp.sum(message * p0[b, :, here], axis=0, keepdims=True)
                part = offs[b, 0:8, here] * offs[b, 8:16, here] * slot
                acc = acc + part
                parts[b, :, here] = jnp.concatenate(split(part), axis=0)
            total = total + dot(parts[b, :, chunks[g]], sel_t[b, chunks[g], atoms:])
        total = total[0:8] + total[8:16]
        pgrad_out[b, 0] = total[:, :ghosts]
        pgrad_out[b, 1] = total[:, ghosts:]
        start_all(halo(3, b))
        total = jnp.zeros((16, atoms), F32)
        for g in range(groups):
            total = total + dot(parts[b, :, chunks[g]], sel_t[b, chunks[g], :atoms])
        fown[b] = total[0:8] + total[8:16] - acc

    def kick(b):
        arrived = jnp.concatenate([pgrad_in[b, 0], pgrad_in[b, 1]], axis=1)
        placed = dot(jnp.concatenate(split(arrived), axis=0), given[b])
        grad = fown[b] + placed[0:8] + placed[8:16]
        kicked[0, b] = momentum[b] - (0.5 * STEP_DT) * grad[0:4]
        start_all(kicks(b))

    arrive(halo(0, 0))
    arrive(halo(0, 1))
    pl.semaphore_wait(ready.at[0], len(near))
    signal(ready.at[1], far_out)
    layer_zero(0)
    layer_zero(1)
    between(0)
    pl.semaphore_wait(ready.at[1], len(far_out))
    start_all(states())
    between(1)
    arrive(halo(1, 0))
    layer_one(0)
    arrive(halo(1, 1))
    layer_one(1)
    own_scatter(0)
    own_scatter(1)
    arrive(halo(2, 0))
    backward(0)
    arrive(halo(2, 1))
    backward(1)

    keep, drift, spring = ring_tables(beads * n_bead)

    def of_positions(table):
        same = jnp.zeros((3, beads, atoms), F32)
        other = jnp.zeros((3, beads, atoms), F32)
        first = lax.broadcasted_iota(jnp.int32, (3, beads, atoms), 1) == 0
        count = len(table)
        for o in range(n_bead):
            source = coords[...] if o == 0 else state[o]
            same = same + table[(2 * o) % count] * source
            other = other + jnp.where(first, table[(2 * o + 1) % count], table[(2 * o - 1) % count]) * source
        return same + jnp.concatenate([other[:, 1:], other[:, :1]], axis=1)

    arrive(halo(3, 0))
    kick(0)
    arrive(states())
    q_base = of_positions(keep)
    p_base = of_positions(spring)
    arrive(halo(3, 1))
    kick(1)
    q_next = [jnp.zeros((4, atoms), F32)] * beads
    p_next = [jnp.zeros((4, atoms), F32)] * beads
    for c in range(beads):
        arrive(kicks(c))
        for b in range(beads):
            for o in range(n_bead):
                apart = (beads * o + b - c) % len(keep)
                source = kicked[o, c]
                q_next[b] = q_next[b] + drift[apart] * source
                p_next[b] = p_next[b] + keep[apart] * source
    for b in range(beads):
        q_next[b] = q_next[b] / mass
        for c in range(3):
            out_q[c, b : b + 1, :] = q_base[c, b : b + 1] + q_next[b][c : c + 1, :]
            out_p[c, b : b + 1, :] = p_next[b][c : c + 1, :] - mass * p_base[c, b : b + 1]
    sent = [states()] + [kicks(b) for b in range(beads)]
    sent += [halo(number, b) for number in range(len(halos)) for b in range(beads)]
    for copies in sent:
        for copy in copies:
            copy.wait_send()


def local(
    coords,
    momenta,
    species,
    atom_features,
    neighbours,
    ghost_rows,
    embed,
    w_filter,
    w_value,
    w_out,
    readout,
):
    n_bead, n_space = lax.axis_size("bead"), lax.axis_size("space")
    beads, _, atoms = coords.shape
    slots = neighbours.shape[2]
    ghosts = ghost_rows.shape[1] // 2
    channels = embed.shape[1]
    edges = slots * atoms
    rows = channels + 16
    vmem = pl.BlockSpec(memory_space=pltpu.VMEM)
    big = pltpu.VMEM((beads, channels, edges), F32)
    per_bead = pltpu.VMEM((beads, channels, atoms), F32)
    shape = jax.ShapeDtypeStruct((3, beads, atoms), F32)
    q_next, p_next = pl.pallas_call(
        functools.partial(kernel, n_bead, n_space),
        out_shape=(pltpu.VMEM((3, beads, atoms), F32),) * 2,
        in_specs=[vmem] * 11,
        out_specs=(vmem, vmem),
        scratch_shapes=[
            pltpu.VMEM((beads, 2 * atoms, edges), BF16),
            pltpu.VMEM((beads, edges, 2 * atoms), BF16),
            pltpu.VMEM((beads, atoms, 2 * ghosts), BF16),
            pltpu.VMEM((beads, 2 * ghosts, atoms), BF16),
            pltpu.VMEM((beads, 8, atoms), F32),
            pltpu.VMEM((beads, rows, atoms), BF16),
            pltpu.VMEM((beads, 2, rows, ghosts), BF16),
            pltpu.VMEM((beads, 2, rows, ghosts), BF16),
            pltpu.VMEM((beads, 2, channels, ghosts), BF16),
            pltpu.VMEM((beads, 2, channels, ghosts), BF16),
            pltpu.VMEM((beads, 2, channels, ghosts), BF16),
            pltpu.VMEM((beads, 2, channels, ghosts), BF16),
            pltpu.VMEM((beads, 2, 8, ghosts), F32),
            pltpu.VMEM((beads, 2, 8, ghosts), F32),
            pltpu.VMEM((n_bead, 3, beads, atoms), F32),
            pltpu.VMEM((n_bead, beads, 4, atoms), F32),
            pltpu.VMEM((beads, 4, atoms), F32),
            pltpu.VMEM((beads, 16, edges), F32),
            pltpu.VMEM((beads, 2, 48, edges), BF16),
            big,
            big,
            big,
            big,
            pltpu.VMEM((channels, atoms), F32),
            per_bead,
            per_bead,
            pltpu.VMEM((beads, channels, atoms), BF16),
            pltpu.VMEM((beads, channels, edges), BF16),
            pltpu.VMEM((beads, 16, edges), BF16),
            per_bead,
            per_bead,
            pltpu.VMEM((beads, 1, edges), F32),
            per_bead,
            pltpu.VMEM((beads, 8, atoms), F32),
            pltpu.SemaphoreType.DMA((4, beads, 2)),
            pltpu.SemaphoreType.DMA((4, beads, 2)),
            pltpu.SemaphoreType.DMA((n_bead,)),
            pltpu.SemaphoreType.DMA((n_bead,)),
            pltpu.SemaphoreType.DMA((beads, n_bead)),
            pltpu.SemaphoreType.DMA((beads, n_bead)),
            pltpu.SemaphoreType.REGULAR((2,)),
        ],
        compiler_params=pltpu.CompilerParams(
            collective_id=0, has_side_effects=True, vmem_limit_bytes=58 * 1024 * 1024
        ),
    )(
        jnp.transpose(coords, (1, 0, 2)),
        jnp.transpose(momenta, (1, 0, 2)),
        species.reshape(1, atoms),
        atom_features,
        jnp.transpose(neighbours, (0, 2, 1)),
        ghost_rows,
        embed,
        w_filter,
        w_value,
        w_out,
        readout.reshape(1, channels),
    )
    return jnp.transpose(q_next, (1, 0, 2)), jnp.transpose(p_next, (1, 0, 2))


def solution(mesh):
    placed = (
        P("bead", None, "space"),
        P("bead", None, "space"),
        P("space"),
        P("space", None),
        P("bead", "space", None),
        P("bead", "space"),
        P(),
        P(),
        P(),
        P(),
        P(),
    )
    return jax.shard_map(
        local,
        mesh=mesh,
        in_specs=placed,
        out_specs=(P("bead", None, "space"), P("bead", None, "space")),
        check_vma=False,
    )
```

```python
import functools
import math

import jax
import jax.numpy as jnp
from jax import lax
from jax.experimental import pallas as pl
from jax.experimental.pallas import tpu as pltpu
from jax.sharding import PartitionSpec as P

MASSES = (1.008, 12.011, 14.007, 15.999, 30.974)
STEP_DT = 1.0
OMEGA_P = 0.6
WIDTH = 3.125
SPACING = 0.25
SOFTEN = 0.01

MESH = pl.DeviceIdType.MESH
BF16 = jnp.bfloat16
F32 = jnp.float32
GROUP = 4


def dot(a, b):
    return jnp.dot(a, b, preferred_element_type=F32)


def one_hot(index, places):
    index = jnp.broadcast_to(index, places.shape)
    return jnp.where(index == places, jnp.ones(places.shape, BF16), jnp.zeros(places.shape, BF16))


def split(x):
    hi = x.astype(BF16)
    return hi, (x - hi.astype(F32)).astype(BF16)


def stacked(x):
    hi, lo = split(x)
    return jnp.concatenate([hi, lo, hi], axis=0)


def ring_tables(count):
    omegas = [2.0 * OMEGA_P * math.sin(math.pi * k / count) for k in range(count)]

    def kernel_of(g):
        return [
            sum(g(w) * math.cos(2.0 * math.pi * k * d / count) for k, w in enumerate(omegas)) / count
            for d in range(count)
        ]

    keep = kernel_of(lambda w: math.cos(w * STEP_DT))
    drift = kernel_of(lambda w: math.sin(w * STEP_DT) / w if w > 0.0 else STEP_DT)
    spring = kernel_of(lambda w: w * math.sin(w * STEP_DT))
    return keep, drift, spring


def kernel(
    n_bead,
    n_space,
    coords_hbm,
    momenta_hbm,
    species_hbm,
    feats_hbm,
    nbr_hbm,
    ghost_rows_hbm,
    embed_hbm,
    w_filter_hbm,
    w_value_hbm,
    w_out_hbm,
    readout_hbm,
    out,
    coords,
    momenta,
    species,
    feats,
    nbr,
    ghost_rows,
    embed,
    w_filter,
    w_value,
    w_out,
    readout,
    sel,
    sel_t,
    handed,
    given,
    pos,
    text,
    halo0_out,
    halo0_in,
    halo1_out,
    halo1_in,
    grad_out,
    grad_in,
    pgrad_out,
    pgrad_in,
    state,
    kicked,
    momentum,
    offs,
    rads,
    apart,
    gv,
    p0,
    f1,
    f1_short,
    g1,
    h0,
    h1,
    u0,
    v1,
    back,
    parts,
    dh,
    dms,
    drs,
    dv,
    fown,
    halo_send,
    halo_recv,
    state_send,
    state_recv,
    kick_send,
    kick_recv,
    ready,
    fetch,
):
    beads, atoms = coords.shape[1:]
    ghosts = ghost_rows.shape[1] // 2
    channels = feats.shape[1]
    slots = nbr.shape[1]
    groups = slots // GROUP
    wide = GROUP * atoms
    me_b = lax.axis_index("bead")
    me_s = lax.axis_index("space")
    left = lax.rem(me_s + n_space - 1, n_space)
    right = lax.rem(me_s + 1, n_space)

    def signal(semaphore, offsets):
        for o in offsets:
            peer = lax.rem(me_b + (o % n_bead), n_bead)
            pl.semaphore_signal(semaphore, inc=1, device_id={"bead": peer}, device_id_type=MESH)

    fetched = dict(
        (name, pltpu.make_async_copy(source, here, fetch.at[i]))
        for i, (name, source, here) in enumerate(
            (
                ("feats", feats_hbm, feats),
                ("species", species_hbm, species),
                ("embed", embed_hbm, embed),
                ("w_value", w_value_hbm, w_value),
                ("ghost_rows", ghost_rows_hbm, ghost_rows),
                ("coords", coords_hbm, coords),
                ("nbr", nbr_hbm, nbr),
                ("w_filter", w_filter_hbm, w_filter),
                ("w_out", w_out_hbm, w_out),
                ("readout", readout_hbm, readout),
                ("momenta", momenta_hbm, momenta),
            )
        )
    )

    def fetch_done(*names):
        for name in names:
            fetched[name].wait()

    near, far_out = (1, -1, 8), (2, -2, 8)
    barrier = pltpu.get_barrier_semaphore()
    for side in (left, right):
        pl.semaphore_signal(barrier, inc=1, device_id={"space": side}, device_id_type=MESH)
    signal(barrier, near)
    for copy in fetched.values():
        copy.start()

    halos = ((halo0_out, halo0_in), (halo1_out, halo1_in), (grad_out, grad_in), (pgrad_out, pgrad_in))

    def halo(number, b):
        src, dst = halos[number]
        return [
            pltpu.make_async_remote_copy(
                src_ref=src.at[b, mine],
                dst_ref=dst.at[b, 1 - mine],
                send_sem=halo_send.at[number, b, mine],
                recv_sem=halo_recv.at[number, b, 1 - mine],
                device_id={"space": side},
                device_id_type=MESH,
            )
            for mine, side in enumerate((left, right))
        ]

    def to_beads(source, part, send, recv):
        return [
            pltpu.make_async_remote_copy(
                src_ref=source,
                dst_ref=part(o),
                send_sem=send.at[o],
                recv_sem=recv.at[o],
                device_id={"bead": lax.rem(me_b + o, n_bead)},
                device_id_type=MESH,
            )
            for o in outward
        ]

    half = n_bead // 2
    outward = sorted(range(1, n_bead), key=lambda o: -2 * min(o % half, half - o % half) - o // half)

    def states():
        return to_beads(coords, lambda o: state.at[o], state_send, state_recv)

    def kicks(b):
        return to_beads(kicked.at[0, b], lambda o: kicked.at[o, b], kick_send.at[b], kick_recv.at[b])

    def start_all(copies):
        for copy in copies:
            copy.start()

    def arrive(copies):
        for copy in copies:
            copy.wait_recv()

    fetch_done("feats", "species", "embed", "w_value", "ghost_rows", "coords")
    kinds = species[...]
    start = jnp.transpose(feats[...])
    mass = jnp.zeros((1, atoms), F32)
    for e in range(embed.shape[0]):
        column = jnp.transpose(jnp.broadcast_to(embed[e : e + 1, :], (128, channels)))
        column = jnp.concatenate([column] * (atoms // 128), axis=1)
        start = start + jnp.where(kinds == e, column, 0.0)
        mass = jnp.where(kinds == e, MASSES[e], mass)
    h0[...] = start
    hi, lo = split(start)
    wv0_t = jnp.transpose(w_value[0].astype(F32)).astype(BF16)
    values_zero = (dot(wv0_t, hi) + dot(wv0_t, lo)).astype(BF16)

    pos[...] = jnp.zeros_like(pos)
    for b in range(beads):
        for c in range(3):
            pos[b, c : c + 1, :] = coords[c, b : b + 1, :]
    atom_rows = lax.broadcasted_iota(jnp.int32, (atoms, atoms), 0).astype(F32).astype(BF16)
    atom_lanes = lax.broadcasted_iota(jnp.int32, (atoms, atoms), 1).astype(F32).astype(BF16)
    for b in range(beads):
        handed[b] = one_hot(ghost_rows[b : b + 1, :].astype(F32).astype(BF16), atom_rows)
        hi, lo = split(pos[b])
        table = jnp.concatenate([values_zero, hi, lo], axis=0)
        text[b] = table
        picked = dot(table, handed[b]).astype(BF16)
        halo0_out[b, 0] = picked[:, :ghosts]
        halo0_out[b, 1] = picked[:, ghosts:]

    pl.semaphore_wait(barrier, 2 + len(near))
    for b in range(beads):
        start_all(halo(0, b))
    signal(ready.at[0], near)

    fetch_done("nbr")
    for b in range(beads):
        lists = nbr[b].astype(F32)
        halves = [lists.astype(BF16), (lists - float(atoms)).astype(BF16)]
        for s in range(slots):
            here = slice(s * atoms, (s + 1) * atoms)
            for half, value in enumerate(halves):
                sel[b, half * atoms : (half + 1) * atoms, here] = one_hot(value[s : s + 1, :], atom_rows)
        got = dot(text[b], sel[b, :atoms, :])
        gv[b] = got[:channels]
        offs[b] = got[channels:]
    for b in range(beads):
        marks = jnp.broadcast_to(ghost_rows[b : b + 1, :], (8, 2 * ghosts))
        columns = jnp.transpose(jnp.concatenate([nbr[b], marks], axis=0)).astype(F32)
        given[b] = one_hot(columns[:, slots : slots + 1].astype(BF16), atom_lanes)
        for s in range(slots):
            here = slice(s * atoms, (s + 1) * atoms)
            column = jnp.broadcast_to(columns[:, s : s + 1], (atoms, atoms))
            sel_t[b, here, :atoms] = one_hot(column.astype(BF16), atom_lanes)
            sel_t[b, here, atoms:] = one_hot((column - float(atoms)).astype(BF16), atom_lanes)

    fetch_done("w_filter", "w_out", "readout", "momenta")
    def filter_rows(layer):
        hi, lo = split(jnp.transpose(w_filter[layer]))
        return jnp.concatenate([hi, hi, lo], axis=1)

    def transposed(weight):
        return jnp.transpose(weight.astype(F32)).astype(BF16)

    wf = [filter_rows(0), filter_rows(1)]
    wv1_t = transposed(w_value[1])
    wo_t = [transposed(w_out[0]), transposed(w_out[1])]
    read = jnp.transpose(jnp.broadcast_to(readout[...], (128, channels)))
    read = jnp.concatenate([read] * (atoms // 128), axis=1)
    momentum[...] = jnp.zeros_like(momentum)
    for b in range(beads):
        for c in range(3):
            momentum[b, c : c + 1, :] = momenta[c, b : b + 1, :]

    centers = SPACING * lax.broadcasted_iota(jnp.int32, (16, atoms), 0).astype(F32)
    lanes = [slice(s * atoms, (s + 1) * atoms) for s in range(slots)]
    chunks = [slice(g * wide, (g + 1) * wide) for g in range(groups)]

    def slope(x, gate):
        return gate * (1.0 + x * (1.0 - gate))

    def layer_zero(b):
        far = jnp.concatenate([halo0_in[b, 0], halo0_in[b, 1]], axis=1)
        acc = jnp.zeros((channels, atoms), F32)
        for g in range(groups):
            got = dot(far, sel[b, atoms:, chunks[g]])
            for s in range(GROUP):
                here, there = lanes[g * GROUP + s], lanes[s]
                place = got[channels:, there] + offs[b, :, here]
                off = place[0:8] + place[8:16] - pos[b]
                offs[b, 0:8, here] = off
                square = jnp.sum(off * off, axis=0, keepdims=True) + SOFTEN
                inverse = lax.rsqrt(square)
                offs[b, 8:16, here] = jnp.broadcast_to(inverse, (8, atoms))
                t = square * inverse - centers
                apart[b, :, here] = t
                rads[b, :, here] = stacked(jnp.exp(-WIDTH * (t * t)))
                value = got[:channels, there] + gv[b, :, here]
                gv[b, :, here] = value
                acc = acc + dot(wf[0], rads[b, :, here]) * value
        update = dot(wo_t[0], acc.astype(BF16))
        u0[b] = update
        hidden = h0[...] + update * jax.nn.sigmoid(update)
        h1[b] = hidden
        value = dot(wv1_t, hidden.astype(BF16)).astype(BF16)
        v1[b] = value
        picked = dot(value, handed[b]).astype(BF16)
        halo1_out[b, 0] = picked[:, :ghosts]
        halo1_out[b, 1] = picked[:, ghosts:]
        start_all(halo(1, b))

    def between(b):
        for g in range(groups):
            g1[b, :, chunks[g]] = dot(v1[b], sel[b, :atoms, chunks[g]])
        for here in lanes:
            weight = dot(wf[1], rads[b, :, here])
            f1[b, :, here] = weight
            f1_short[b, :, here] = weight.astype(BF16)

    def layer_one(b):
        far = jnp.concatenate([halo1_in[b, 0], halo1_in[b, 1]], axis=1)
        acc = jnp.zeros((channels, atoms), F32)
        for g in range(groups):
            got = dot(far, sel[b, atoms:, chunks[g]])
            for s in range(GROUP):
                here, there = lanes[g * GROUP + s], lanes[s]
                value = g1[b, :, here] + got[:, there]
                acc = acc + f1[b, :, here] * value
                g1[b, :, here] = value
        update = dot(wo_t[1], acc.astype(BF16))
        gate = jax.nn.sigmoid(update)
        hidden = h1[b] + update * gate
        grad = read * slope(hidden, jax.nn.sigmoid(hidden))
        dh[b] = grad
        grad = grad * slope(update, gate)
        message = dot(w_out[1], grad.astype(BF16))
        dms[b] = message
        short = message.astype(BF16)
        total = jnp.zeros((channels, 2 * ghosts), F32)
        for g in range(groups):
            for s in range(GROUP):
                here = lanes[g * GROUP + s]
                back[b, :, here] = f1_short[b, :, here] * short
            total = total + dot(back[b, :, chunks[g]], sel_t[b, chunks[g], atoms:])
        value = total.astype(BF16)
        grad_out[b, 0] = value[:, :ghosts]
        grad_out[b, 1] = value[:, ghosts:]
        start_all(halo(2, b))

    def own_scatter(b):
        total = jnp.zeros((channels, atoms), F32)
        for g in range(groups):
            total = total + dot(back[b, :, chunks[g]], sel_t[b, chunks[g], :atoms])
        dv[b] = total
        for here in lanes:
            t = apart[b, :, here]
            steep = stacked((-2.0 * WIDTH) * (t * jnp.exp(-WIDTH * (t * t))))
            p0[b, :, here] = dot(wf[0], steep) * gv[b, :, here]
            change = dot(wf[1], steep) * g1[b, :, here]
            drs[b, :, here] = jnp.sum(dms[b] * change, axis=0, keepdims=True)

    def backward(b):
        arrived = jnp.concatenate([grad_in[b, 0], grad_in[b, 1]], axis=1)
        value = dv[b] + dot(arrived, given[b])
        grad = dh[b] + dot(w_value[1], value.astype(BF16))
        update = u0[b]
        grad = grad * slope(update, jax.nn.sigmoid(update))
        message = dot(w_out[0], grad.astype(BF16))
        acc = jnp.zeros((8, atoms), F32)
        total = jnp.zeros((16, 2 * ghosts), F32)
        for g in range(groups):
            for s in range(GROUP):
                here = lanes[g * GROUP + s]
                slot = drs[b, :, here] + jnp.sum(message * p0[b, :, here], axis=0, keepdims=True)
                part = offs[b, 0:8, here] * offs[b, 8:16, here] * slot
                acc = acc + part
                parts[b, :, here] = jnp.concatenate(split(part), axis=0)
            total = total + dot(parts[b, :, chunks[g]], sel_t[b, chunks[g], atoms:])
        total = total[0:8] + total[8:16]
        pgrad_out[b, 0] = total[:, :ghosts]
        pgrad_out[b, 1] = total[:, ghosts:]
        start_all(halo(3, b))
        total = jnp.zeros((16, atoms), F32)
        for g in range(groups):
            total = total + dot(parts[b, :, chunks[g]], sel_t[b, chunks[g], :atoms])
        fown[b] = total[0:8] + total[8:16] - acc

    def kick(b):
        arrived = jnp.concatenate([pgrad_in[b, 0], pgrad_in[b, 1]], axis=1)
        placed = dot(jnp.concatenate(split(arrived), axis=0), given[b])
        grad = fown[b] + placed[0:8] + placed[8:16]
        kicked[0, b] = momentum[b] - (0.5 * STEP_DT) * grad[0:4]
        start_all(kicks(b))

    arrive(halo(0, 0))
    arrive(halo(0, 1))
    pl.semaphore_wait(ready.at[0], len(near))
    signal(ready.at[1], far_out)
    layer_zero(0)
    layer_zero(1)
    between(0)
    pl.semaphore_wait(ready.at[1], len(far_out))
    start_all(states())
    between(1)
    arrive(halo(1, 0))
    layer_one(0)
    arrive(halo(1, 1))
    layer_one(1)
    own_scatter(0)
    own_scatter(1)
    arrive(halo(2, 0))
    backward(0)
    arrive(halo(2, 1))
    backward(1)

    keep, drift, spring = ring_tables(beads * n_bead)

    def of_positions(table):
        same = jnp.zeros((3, beads, atoms), F32)
        other = jnp.zeros((3, beads, atoms), F32)
        first = lax.broadcasted_iota(jnp.int32, (3, beads, atoms), 1) == 0
        count = len(table)
        for o in range(n_bead):
            source = coords[...] if o == 0 else state[o]
            same = same + table[(2 * o) % count] * source
            other = other + jnp.where(first, table[(2 * o + 1) % count], table[(2 * o - 1) % count]) * source
        return same + jnp.concatenate([other[:, 1:], other[:, :1]], axis=1)

    arrive(halo(3, 0))
    kick(0)
    arrive(states())
    q_base = of_positions(keep)
    p_base = of_positions(spring)
    inverse_mass = 1.0 / mass
    arrive(halo(3, 1))
    kick(1)
    q_next = [jnp.zeros((4, atoms), F32)] * beads
    p_next = [jnp.zeros((4, atoms), F32)] * beads
    for c in range(beads):
        arrivals = kicks(c)
        for o in [0] + outward[::-1]:
            if o:
                arrivals[outward.index(o)].wait_recv()
            source = kicked[o, c]
            for b in range(beads):
                d = (beads * o + b - c) % len(keep)
                q_next[b] = q_next[b] + drift[d] * source
                p_next[b] = p_next[b] + keep[d] * source
    for b in range(beads):
        q_next[b] = q_next[b] * inverse_mass
        for c in range(3):
            out[0, c, b : b + 1, :] = q_base[c, b : b + 1] + q_next[b][c : c + 1, :]
            out[1, c, b : b + 1, :] = p_next[b][c : c + 1, :] - mass * p_base[c, b : b + 1]
    sent = [states()] + [kicks(b) for b in range(beads)]
    sent += [halo(number, b) for number in range(len(halos)) for b in range(beads)]
    for copies in sent:
        for copy in copies:
            copy.wait_send()


def local(
    coords,
    momenta,
    species,
    atom_features,
    neighbours,
    ghost_rows,
    embed,
    w_filter,
    w_value,
    w_out,
    readout,
):
    n_bead, n_space = lax.axis_size("bead"), lax.axis_size("space")
    beads, _, atoms = coords.shape
    slots = neighbours.shape[2]
    ghosts = ghost_rows.shape[1] // 2
    channels = embed.shape[1]
    edges = slots * atoms
    rows = channels + 16
    vmem = pl.BlockSpec(memory_space=pltpu.VMEM)
    big = pltpu.VMEM((beads, channels, edges), F32)
    per_bead = pltpu.VMEM((beads, channels, atoms), F32)
    shape = jax.ShapeDtypeStruct((3, beads, atoms), F32)
    result = pl.pallas_call(
        functools.partial(kernel, n_bead, n_space),
        out_shape=pltpu.VMEM((2, 3, beads, atoms), F32),
        in_specs=[pl.BlockSpec(memory_space=pl.ANY)] * 11,
        out_specs=vmem,
        scratch_shapes=[
            pltpu.VMEM((3, beads, atoms), F32),
            pltpu.VMEM((3, beads, atoms), F32),
            pltpu.VMEM((1, atoms), jnp.int32),
            pltpu.VMEM(atom_features.shape, F32),
            pltpu.VMEM((beads, slots, atoms), jnp.int32),
            pltpu.VMEM(ghost_rows.shape, jnp.int32),
            pltpu.VMEM(embed.shape, F32),
            pltpu.VMEM(w_filter.shape, F32),
            pltpu.VMEM(w_value.shape, BF16),
            pltpu.VMEM(w_out.shape, BF16),
            pltpu.VMEM((1, channels), F32),
            pltpu.VMEM((beads, 2 * atoms, edges), BF16),
            pltpu.VMEM((beads, edges, 2 * atoms), BF16),
            pltpu.VMEM((beads, atoms, 2 * ghosts), BF16),
            pltpu.VMEM((beads, 2 * ghosts, atoms), BF16),
            pltpu.VMEM((beads, 8, atoms), F32),
            pltpu.VMEM((beads, rows, atoms), BF16),
            pltpu.VMEM((beads, 2, rows, ghosts), BF16),
            pltpu.VMEM((beads, 2, rows, ghosts), BF16),
            pltpu.VMEM((beads, 2, channels, ghosts), BF16),
            pltpu.VMEM((beads, 2, channels, ghosts), BF16),
            pltpu.VMEM((beads, 2, channels, ghosts), BF16),
            pltpu.VMEM((beads, 2, channels, ghosts), BF16),
            pltpu.VMEM((beads, 2, 8, ghosts), F32),
            pltpu.VMEM((beads, 2, 8, ghosts), F32),
            pltpu.VMEM((n_bead, 3, beads, atoms), F32),
            pltpu.VMEM((n_bead, beads, 4, atoms), F32),
            pltpu.VMEM((beads, 4, atoms), F32),
            pltpu.VMEM((beads, 16, edges), F32),
            pltpu.VMEM((beads, 48, edges), BF16),
            pltpu.VMEM((beads, 16, edges), F32),
            big,
            big,
            big,
            pltpu.VMEM((beads, channels, edges), BF16),
            big,
            pltpu.VMEM((channels, atoms), F32),
            per_bead,
            per_bead,
            pltpu.VMEM((beads, channels, atoms), BF16),
            pltpu.VMEM((beads, channels, edges), BF16),
            pltpu.VMEM((beads, 16, edges), BF16),
            per_bead,
            per_bead,
            pltpu.VMEM((beads, 1, edges), F32),
            per_bead,
            pltpu.VMEM((beads, 8, atoms), F32),
            pltpu.SemaphoreType.DMA((4, beads, 2)),
            pltpu.SemaphoreType.DMA((4, beads, 2)),
            pltpu.SemaphoreType.DMA((n_bead,)),
            pltpu.SemaphoreType.DMA((n_bead,)),
            pltpu.SemaphoreType.DMA((beads, n_bead)),
            pltpu.SemaphoreType.DMA((beads, n_bead)),
            pltpu.SemaphoreType.REGULAR((2,)),
            pltpu.SemaphoreType.DMA((11,)),
        ],
        compiler_params=pltpu.CompilerParams(
            collective_id=0, has_side_effects=True, vmem_limit_bytes=60 * 1024 * 1024
        ),
    )(
        jnp.transpose(coords, (1, 0, 2)),
        jnp.transpose(momenta, (1, 0, 2)),
        species.reshape(1, atoms),
        atom_features,
        jnp.transpose(neighbours, (0, 2, 1)),
        ghost_rows,
        embed,
        w_filter,
        w_value,
        w_out,
        readout.reshape(1, channels),
    )
    return jnp.transpose(result[0], (1, 0, 2)), jnp.transpose(result[1], (1, 0, 2))


def solution(mesh):
    placed = (
        P("bead", None, "space"),
        P("bead", None, "space"),
        P("space"),
        P("space", None),
        P("bead", "space", None),
        P("bead", "space"),
        P(),
        P(),
        P(),
        P(),
        P(),
    )
    return jax.shard_map(
        local,
        mesh=mesh,
        in_specs=placed,
        out_specs=(P("bead", None, "space"), P("bead", None, "space")),
        check_vma=False,
    )
```

```python
import functools
import math

import jax
import jax.numpy as jnp
from jax import lax
from jax.experimental import pallas as pl
from jax.experimental.pallas import tpu as pltpu
from jax.sharding import PartitionSpec as P

MASSES = (1.008, 12.011, 14.007, 15.999, 30.974)
STEP_DT = 1.0
OMEGA_P = 0.6
WIDTH = 3.125
SPACING = 0.25
SOFTEN = 0.01

MESH = pl.DeviceIdType.MESH
BF16 = jnp.bfloat16
F32 = jnp.float32
GROUP = 4


def dot(a, b):
    return jnp.dot(a, b, preferred_element_type=F32)


def one_hot(index, places):
    index = jnp.broadcast_to(index, places.shape)
    return jnp.where(index == places, jnp.ones(places.shape, BF16), jnp.zeros(places.shape, BF16))


def split(x):
    hi = x.astype(BF16)
    return hi, (x - hi.astype(F32)).astype(BF16)


def stacked(x):
    hi, lo = split(x)
    return jnp.concatenate([hi, lo, hi], axis=0)


def ring_tables(count):
    omegas = [2.0 * OMEGA_P * math.sin(math.pi * k / count) for k in range(count)]

    def kernel_of(g):
        return [
            sum(g(w) * math.cos(2.0 * math.pi * k * d / count) for k, w in enumerate(omegas)) / count
            for d in range(count)
        ]

    keep = kernel_of(lambda w: math.cos(w * STEP_DT))
    drift = kernel_of(lambda w: math.sin(w * STEP_DT) / w if w > 0.0 else STEP_DT)
    spring = kernel_of(lambda w: w * math.sin(w * STEP_DT))
    return keep, drift, spring


def kernel(
    n_bead,
    n_space,
    coords_hbm,
    momenta_hbm,
    species_hbm,
    feats_hbm,
    nbr_hbm,
    ghost_rows_hbm,
    embed_hbm,
    w_filter_hbm,
    w_value_hbm,
    w_out_hbm,
    readout_hbm,
    out,
    coords,
    momenta,
    species,
    feats,
    nbr,
    ghost_rows,
    embed,
    w_filter,
    w_value,
    w_out,
    readout,
    sel,
    sel_t,
    handed,
    given,
    pos,
    text,
    halo0_out,
    halo0_in,
    halo1_out,
    halo1_in,
    grad_out,
    grad_in,
    pgrad_out,
    pgrad_in,
    state,
    kicked,
    momentum,
    offs,
    rads,
    apart,
    gv,
    p0,
    f1,
    f1_short,
    g1,
    h0,
    h1,
    u0,
    v1,
    back,
    parts,
    dh,
    dms,
    drs,
    dv,
    fown,
    halo_send,
    halo_recv,
    state_send,
    state_recv,
    kick_send,
    kick_recv,
    ready,
    fetch,
):
    beads, atoms = coords.shape[1:]
    ghosts = ghost_rows.shape[1] // 2
    channels = feats.shape[1]
    slots = nbr.shape[1]
    groups = slots // GROUP
    wide = GROUP * atoms
    me_b = lax.axis_index("bead")
    me_s = lax.axis_index("space")
    left = lax.rem(me_s + n_space - 1, n_space)
    right = lax.rem(me_s + 1, n_space)

    def signal(semaphore, offsets):
        for o in offsets:
            peer = lax.rem(me_b + (o % n_bead), n_bead)
            pl.semaphore_signal(semaphore, inc=1, device_id={"bead": peer}, device_id_type=MESH)

    fetched = dict(
        (name, pltpu.make_async_copy(source, here, fetch.at[i]))
        for i, (name, source, here) in enumerate(
            (
                ("feats", feats_hbm, feats),
                ("species", species_hbm, species),
                ("embed", embed_hbm, embed),
                ("w_value", w_value_hbm, w_value),
                ("ghost_rows", ghost_rows_hbm, ghost_rows),
                ("coords", coords_hbm, coords),
                ("nbr", nbr_hbm, nbr),
                ("w_filter", w_filter_hbm, w_filter),
                ("w_out", w_out_hbm, w_out),
                ("readout", readout_hbm, readout),
                ("momenta", momenta_hbm, momenta),
            )
        )
    )

    def fetch_done(*names):
        for name in names:
            fetched[name].wait()

    near, far_out = (1, -1, 8), (2, -2, 8)
    barrier = pltpu.get_barrier_semaphore()
    for side in (left, right):
        pl.semaphore_signal(barrier, inc=1, device_id={"space": side}, device_id_type=MESH)
    signal(barrier, near)
    for copy in fetched.values():
        copy.start()

    halos = ((halo0_out, halo0_in), (halo1_out, halo1_in), (grad_out, grad_in), (pgrad_out, pgrad_in))

    def halo(number, b):
        src, dst = halos[number]
        return [
            pltpu.make_async_remote_copy(
                src_ref=src.at[b, mine],
                dst_ref=dst.at[b, 1 - mine],
                send_sem=halo_send.at[number, b, mine],
                recv_sem=halo_recv.at[number, b, 1 - mine],
                device_id={"space": side},
                device_id_type=MESH,
            )
            for mine, side in enumerate((left, right))
        ]

    def to_beads(source, part, send, recv):
        return [
            pltpu.make_async_remote_copy(
                src_ref=source,
                dst_ref=part(o),
                send_sem=send.at[o],
                recv_sem=recv.at[o],
                device_id={"bead": lax.rem(me_b + o, n_bead)},
                device_id_type=MESH,
            )
            for o in outward
        ]

    half = n_bead // 2
    outward = sorted(range(1, n_bead), key=lambda o: -2 * min(o % half, half - o % half) - o // half)

    def states():
        return to_beads(coords, lambda o: state.at[o], state_send, state_recv)

    def kicks(b):
        return to_beads(kicked.at[0, b], lambda o: kicked.at[o, b], kick_send.at[b], kick_recv.at[b])

    def start_all(copies):
        for copy in copies:
            copy.start()

    def arrive(copies):
        for copy in copies:
            copy.wait_recv()

    fetch_done("feats", "species", "embed", "w_value", "ghost_rows", "coords")
    kinds = species[...]
    start = jnp.transpose(feats[...])
    mass = jnp.zeros((1, atoms), F32)
    for e in range(embed.shape[0]):
        column = jnp.transpose(jnp.broadcast_to(embed[e : e + 1, :], (128, channels)))
        column = jnp.concatenate([column] * (atoms // 128), axis=1)
        start = start + jnp.where(kinds == e, column, 0.0)
        mass = jnp.where(kinds == e, MASSES[e], mass)
    h0[...] = start
    hi, lo = split(start)
    wv0_t = jnp.transpose(w_value[0].astype(F32)).astype(BF16)
    values_zero = (dot(wv0_t, hi) + dot(wv0_t, lo)).astype(BF16)

    pos[...] = jnp.zeros_like(pos)
    for b in range(beads):
        for c in range(3):
            pos[b, c : c + 1, :] = coords[c, b : b + 1, :]
    atom_rows = lax.broadcasted_iota(jnp.int32, (atoms, atoms), 0).astype(F32).astype(BF16)
    atom_lanes = lax.broadcasted_iota(jnp.int32, (atoms, atoms), 1).astype(F32).astype(BF16)
    for b in range(beads):
        handed[b] = one_hot(ghost_rows[b : b + 1, :].astype(F32).astype(BF16), atom_rows)
        hi, lo = split(pos[b])
        table = jnp.concatenate([values_zero, hi, lo], axis=0)
        text[b] = table
        picked = dot(table, handed[b]).astype(BF16)
        halo0_out[b, 0] = picked[:, :ghosts]
        halo0_out[b, 1] = picked[:, ghosts:]

    pl.semaphore_wait(barrier, 2 + len(near))
    for b in range(beads):
        start_all(halo(0, b))
    signal(ready.at[0], near)

    fetch_done("nbr")
    for b in range(beads):
        lists = nbr[b].astype(F32)
        halves = [lists.astype(BF16), (lists - float(atoms)).astype(BF16)]
        for s in range(slots):
            here = slice(s * atoms, (s + 1) * atoms)
            for half, value in enumerate(halves):
                sel[b, half * atoms : (half + 1) * atoms, here] = one_hot(value[s : s + 1, :], atom_rows)
        got = dot(text[b], sel[b, :atoms, :])
        gv[b] = got[:channels]
        offs[b] = got[channels:]
    for b in range(beads):
        marks = jnp.broadcast_to(ghost_rows[b : b + 1, :], (8, 2 * ghosts))
        columns = jnp.transpose(jnp.concatenate([nbr[b], marks], axis=0)).astype(F32)
        given[b] = one_hot(columns[:, slots : slots + 1].astype(BF16), atom_lanes)
        for s in range(slots):
            here = slice(s * atoms, (s + 1) * atoms)
            column = jnp.broadcast_to(columns[:, s : s + 1], (atoms, atoms))
            sel_t[b, here, :atoms] = one_hot(column.astype(BF16), atom_lanes)
            sel_t[b, here, atoms:] = one_hot((column - float(atoms)).astype(BF16), atom_lanes)

    fetch_done("w_filter", "w_out", "readout", "momenta")
    def filter_rows(layer):
        hi, lo = split(jnp.transpose(w_filter[layer]))
        return jnp.concatenate([hi, hi, lo], axis=1)

    def transposed(weight):
        return jnp.transpose(weight.astype(F32)).astype(BF16)

    wf = [filter_rows(0), filter_rows(1)]
    wv1_t = transposed(w_value[1])
    wo_t = [transposed(w_out[0]), transposed(w_out[1])]
    read = jnp.transpose(jnp.broadcast_to(readout[...], (128, channels)))
    read = jnp.concatenate([read] * (atoms // 128), axis=1)
    momentum[...] = jnp.zeros_like(momentum)
    for b in range(beads):
        for c in range(3):
            momentum[b, c : c + 1, :] = momenta[c, b : b + 1, :]

    centers = SPACING * lax.broadcasted_iota(jnp.int32, (16, atoms), 0).astype(F32)
    lanes = [slice(s * atoms, (s + 1) * atoms) for s in range(slots)]
    chunks = [slice(g * wide, (g + 1) * wide) for g in range(groups)]

    def slope(x, gate):
        return gate * (1.0 + x * (1.0 - gate))

    def layer_zero(b):
        far = jnp.concatenate([halo0_in[b, 0], halo0_in[b, 1]], axis=1)
        for g in range(groups):
            here = chunks[g]
            got = dot(far, sel[b, atoms:, here])
            place = got[channels:] + offs[b, :, here]
            offs[b, 0:8, here] = place[0:8] + place[8:16]
            gv[b, :, here] = gv[b, :, here] + got[:channels]
        for here in lanes:
            off = offs[b, 0:8, here] - pos[b]
            offs[b, 0:8, here] = off
            square = jnp.sum(off * off, axis=0, keepdims=True) + SOFTEN
            inverse = lax.rsqrt(square)
            offs[b, 8:16, here] = jnp.broadcast_to(inverse, (8, atoms))
            t = square * inverse - centers
            apart[b, :, here] = t
            rads[b, :, here] = stacked(jnp.exp(-WIDTH * (t * t)))
        acc = jnp.zeros((channels, atoms), F32)
        for g in range(groups):
            weight = dot(wf[0], rads[b, :, chunks[g]])
            for s in range(GROUP):
                acc = acc + weight[:, lanes[s]] * gv[b, :, lanes[g * GROUP + s]]
        update = dot(wo_t[0], acc.astype(BF16))
        u0[b] = update
        hidden = h0[...] + update * jax.nn.sigmoid(update)
        h1[b] = hidden
        value = dot(wv1_t, hidden.astype(BF16)).astype(BF16)
        v1[b] = value
        picked = dot(value, handed[b]).astype(BF16)
        halo1_out[b, 0] = picked[:, :ghosts]
        halo1_out[b, 1] = picked[:, ghosts:]
        start_all(halo(1, b))

    def between(b):
        for g in range(groups):
            g1[b, :, chunks[g]] = dot(v1[b], sel[b, :atoms, chunks[g]])
        for here in lanes:
            weight = dot(wf[1], rads[b, :, here])
            f1[b, :, here] = weight
            f1_short[b, :, here] = weight.astype(BF16)

    def layer_one(b):
        far = jnp.concatenate([halo1_in[b, 0], halo1_in[b, 1]], axis=1)
        acc = jnp.zeros((channels, atoms), F32)
        for g in range(groups):
            got = dot(far, sel[b, atoms:, chunks[g]])
            for s in range(GROUP):
                here, there = lanes[g * GROUP + s], lanes[s]
                value = g1[b, :, here] + got[:, there]
                acc = acc + f1[b, :, here] * value
                g1[b, :, here] = value
        update = dot(wo_t[1], acc.astype(BF16))
        gate = jax.nn.sigmoid(update)
        hidden = h1[b] + update * gate
        grad = read * slope(hidden, jax.nn.sigmoid(hidden))
        dh[b] = grad
        grad = grad * slope(update, gate)
        message = dot(w_out[1], grad.astype(BF16))
        dms[b] = message
        short = message.astype(BF16)
        for here in lanes:
            back[b, :, here] = f1_short[b, :, here] * short
        value = dot(back[b], sel_t[b, :, atoms:]).astype(BF16)
        grad_out[b, 0] = value[:, :ghosts]
        grad_out[b, 1] = value[:, ghosts:]
        start_all(halo(2, b))

    def own_scatter(b):
        dv[b] = dot(back[b], sel_t[b, :, :atoms])
        for here in lanes:
            t = apart[b, :, here]
            steep = stacked((-2.0 * WIDTH) * (t * jnp.exp(-WIDTH * (t * t))))
            p0[b, :, here] = dot(wf[0], steep) * gv[b, :, here]
            change = dot(wf[1], steep) * g1[b, :, here]
            drs[b, :, here] = jnp.sum(dms[b] * change, axis=0, keepdims=True)

    def backward(b):
        arrived = jnp.concatenate([grad_in[b, 0], grad_in[b, 1]], axis=1)
        value = dv[b] + dot(arrived, given[b])
        grad = dh[b] + dot(w_value[1], value.astype(BF16))
        update = u0[b]
        grad = grad * slope(update, jax.nn.sigmoid(update))
        message = dot(w_out[0], grad.astype(BF16))
        acc = jnp.zeros((8, atoms), F32)
        for here in lanes:
                slot = drs[b, :, here] + jnp.sum(message * p0[b, :, here], axis=0, keepdims=True)
                part = offs[b, 0:8, here] * offs[b, 8:16, here] * slot
                acc = acc + part
                parts[b, :, here] = jnp.concatenate(split(part), axis=0)
        total = dot(parts[b], sel_t[b, :, atoms:])
        total = total[0:8] + total[8:16]
        pgrad_out[b, 0] = total[:, :ghosts]
        pgrad_out[b, 1] = total[:, ghosts:]
        start_all(halo(3, b))
        total = dot(parts[b], sel_t[b, :, :atoms])
        fown[b] = total[0:8] + total[8:16] - acc

    def kick(b):
        arrived = jnp.concatenate([pgrad_in[b, 0], pgrad_in[b, 1]], axis=1)
        placed = dot(jnp.concatenate(split(arrived), axis=0), given[b])
        grad = fown[b] + placed[0:8] + placed[8:16]
        kicked[0, b] = momentum[b] - (0.5 * STEP_DT) * grad[0:4]
        start_all(kicks(b))

    arrive(halo(0, 0))
    arrive(halo(0, 1))
    pl.semaphore_wait(ready.at[0], len(near))
    signal(ready.at[1], far_out)
    layer_zero(0)
    layer_zero(1)
    between(0)
    pl.semaphore_wait(ready.at[1], len(far_out))
    start_all(states())
    between(1)
    arrive(halo(1, 0))
    layer_one(0)
    arrive(halo(1, 1))
    layer_one(1)
    own_scatter(0)
    own_scatter(1)
    arrive(halo(2, 0))
    backward(0)
    arrive(halo(2, 1))
    backward(1)

    keep, drift, spring = ring_tables(beads * n_bead)

    def of_positions(table):
        same = jnp.zeros((3, beads, atoms), F32)
        other = jnp.zeros((3, beads, atoms), F32)
        first = lax.broadcasted_iota(jnp.int32, (3, beads, atoms), 1) == 0
        count = len(table)
        for o in range(n_bead):
            source = coords[...] if o == 0 else state[o]
            same = same + table[(2 * o) % count] * source
            other = other + jnp.where(first, table[(2 * o + 1) % count], table[(2 * o - 1) % count]) * source
        return same + jnp.concatenate([other[:, 1:], other[:, :1]], axis=1)

    arrive(halo(3, 0))
    kick(0)
    arrive(states())
    q_base = of_positions(keep)
    p_base = of_positions(spring)
    inverse_mass = 1.0 / mass
    arrive(halo(3, 1))
    kick(1)
    sent = [states()] + [kicks(b) for b in range(beads)]
    sent += [halo(number, b) for number in range(len(halos)) for b in range(beads)]
    for copies in sent:
        for copy in copies:
            copy.wait_send()
    q_next = [jnp.zeros((4, atoms), F32)] * beads
    p_next = [jnp.zeros((4, atoms), F32)] * beads
    for c in range(beads):
        arrivals = kicks(c)
        for o in [0] + outward[::-1]:
            if o:
                arrivals[outward.index(o)].wait_recv()
            source = kicked[o, c]
            for b in range(beads):
                d = (beads * o + b - c) % len(keep)
                q_next[b] = q_next[b] + drift[d] * source
                p_next[b] = p_next[b] + keep[d] * source
    for b in range(beads):
        q_next[b] = q_next[b] * inverse_mass
        for c in range(3):
            out[0, c, b : b + 1, :] = q_base[c, b : b + 1] + q_next[b][c : c + 1, :]
            out[1, c, b : b + 1, :] = p_next[b][c : c + 1, :] - mass * p_base[c, b : b + 1]


def local(
    coords,
    momenta,
    species,
    atom_features,
    neighbours,
    ghost_rows,
    embed,
    w_filter,
    w_value,
    w_out,
    readout,
):
    n_bead, n_space = lax.axis_size("bead"), lax.axis_size("space")
    beads, _, atoms = coords.shape
    slots = neighbours.shape[2]
    ghosts = ghost_rows.shape[1] // 2
    channels = embed.shape[1]
    edges = slots * atoms
    rows = channels + 16
    vmem = pl.BlockSpec(memory_space=pltpu.VMEM)
    big = pltpu.VMEM((beads, channels, edges), F32)
    per_bead = pltpu.VMEM((beads, channels, atoms), F32)
    shape = jax.ShapeDtypeStruct((3, beads, atoms), F32)
    result = pl.pallas_call(
        functools.partial(kernel, n_bead, n_space),
        out_shape=pltpu.VMEM((2, 3, beads, atoms), F32),
        in_specs=[pl.BlockSpec(memory_space=pl.ANY)] * 11,
        out_specs=vmem,
        scratch_shapes=[
            pltpu.VMEM((3, beads, atoms), F32),
            pltpu.VMEM((3, beads, atoms), F32),
            pltpu.VMEM((1, atoms), jnp.int32),
            pltpu.VMEM(atom_features.shape, F32),
            pltpu.VMEM((beads, slots, atoms), jnp.int32),
            pltpu.VMEM(ghost_rows.shape, jnp.int32),
            pltpu.VMEM(embed.shape, F32),
            pltpu.VMEM(w_filter.shape, F32),
            pltpu.VMEM(w_value.shape, BF16),
            pltpu.VMEM(w_out.shape, BF16),
            pltpu.VMEM((1, channels), F32),
            pltpu.VMEM((beads, 2 * atoms, edges), BF16),
            pltpu.VMEM((beads, edges, 2 * atoms), BF16),
            pltpu.VMEM((beads, atoms, 2 * ghosts), BF16),
            pltpu.VMEM((beads, 2 * ghosts, atoms), BF16),
            pltpu.VMEM((beads, 8, atoms), F32),
            pltpu.VMEM((beads, rows, atoms), BF16),
            pltpu.VMEM((beads, 2, rows, ghosts), BF16),
            pltpu.VMEM((beads, 2, rows, ghosts), BF16),
            pltpu.VMEM((beads, 2, channels, ghosts), BF16),
            pltpu.VMEM((beads, 2, channels, ghosts), BF16),
            pltpu.VMEM((beads, 2, channels, ghosts), BF16),
            pltpu.VMEM((beads, 2, channels, ghosts), BF16),
            pltpu.VMEM((beads, 2, 8, ghosts), F32),
            pltpu.VMEM((beads, 2, 8, ghosts), F32),
            pltpu.VMEM((n_bead, 3, beads, atoms), F32),
            pltpu.VMEM((n_bead, beads, 4, atoms), F32),
            pltpu.VMEM((beads, 4, atoms), F32),
            pltpu.VMEM((beads, 16, edges), F32),
            pltpu.VMEM((beads, 48, edges), BF16),
            pltpu.VMEM((beads, 16, edges), F32),
            big,
            big,
            big,
            pltpu.VMEM((beads, channels, edges), BF16),
            big,
            pltpu.VMEM((channels, atoms), F32),
            per_bead,
            per_bead,
            pltpu.VMEM((beads, channels, atoms), BF16),
            pltpu.VMEM((beads, channels, edges), BF16),
            pltpu.VMEM((beads, 16, edges), BF16),
            per_bead,
            per_bead,
            pltpu.VMEM((beads, 1, edges), F32),
            per_bead,
            pltpu.VMEM((beads, 8, atoms), F32),
            pltpu.SemaphoreType.DMA((4, beads, 2)),
            pltpu.SemaphoreType.DMA((4, beads, 2)),
            pltpu.SemaphoreType.DMA((n_bead,)),
            pltpu.SemaphoreType.DMA((n_bead,)),
            pltpu.SemaphoreType.DMA((beads, n_bead)),
            pltpu.SemaphoreType.DMA((beads, n_bead)),
            pltpu.SemaphoreType.REGULAR((2,)),
            pltpu.SemaphoreType.DMA((11,)),
        ],
        compiler_params=pltpu.CompilerParams(
            collective_id=0, has_side_effects=True, vmem_limit_bytes=60 * 1024 * 1024
        ),
    )(
        jnp.transpose(coords, (1, 0, 2)),
        jnp.transpose(momenta, (1, 0, 2)),
        species.reshape(1, atoms),
        atom_features,
        jnp.transpose(neighbours, (0, 2, 1)),
        ghost_rows,
        embed,
        w_filter,
        w_value,
        w_out,
        readout.reshape(1, channels),
    )
    return jnp.transpose(result[0], (1, 0, 2)), jnp.transpose(result[1], (1, 0, 2))


def solution(mesh):
    placed = (
        P("bead", None, "space"),
        P("bead", None, "space"),
        P("space"),
        P("space", None),
        P("bead", "space", None),
        P("bead", "space"),
        P(),
        P(),
        P(),
        P(),
        P(),
    )
    return jax.shard_map(
        local,
        mesh=mesh,
        in_specs=placed,
        out_specs=(P("bead", None, "space"), P("bead", None, "space")),
        check_vma=False,
    )
```

```python
import functools
import math

import jax
import jax.numpy as jnp
from jax import lax
from jax.experimental import pallas as pl
from jax.experimental.pallas import tpu as pltpu
from jax.sharding import PartitionSpec as P

MASSES = (1.008, 12.011, 14.007, 15.999, 30.974)
STEP_DT = 1.0
OMEGA_P = 0.6
WIDTH = 3.125
SPACING = 0.25
SOFTEN = 0.01

MESH = pl.DeviceIdType.MESH
BF16 = jnp.bfloat16
F32 = jnp.float32
GROUP = 4


def dot(a, b):
    return jnp.dot(a, b, preferred_element_type=F32)


def one_hot(index, places):
    index = jnp.broadcast_to(index, places.shape)
    return jnp.where(index == places, jnp.ones(places.shape, BF16), jnp.zeros(places.shape, BF16))


def split(x):
    hi = x.astype(BF16)
    return hi, (x - hi.astype(F32)).astype(BF16)


def stacked(x):
    hi, lo = split(x)
    return jnp.concatenate([hi, lo, hi], axis=0)


def ring_tables(count):
    omegas = [2.0 * OMEGA_P * math.sin(math.pi * k / count) for k in range(count)]

    def kernel_of(g):
        return [
            sum(g(w) * math.cos(2.0 * math.pi * k * d / count) for k, w in enumerate(omegas)) / count
            for d in range(count)
        ]

    keep = kernel_of(lambda w: math.cos(w * STEP_DT))
    drift = kernel_of(lambda w: math.sin(w * STEP_DT) / w if w > 0.0 else STEP_DT)
    spring = kernel_of(lambda w: w * math.sin(w * STEP_DT))
    return keep, drift, spring


def kernel(
    n_bead,
    n_space,
    coords_hbm,
    momenta_hbm,
    species_hbm,
    feats_hbm,
    nbr_hbm,
    ghost_rows_hbm,
    embed_hbm,
    w_filter_hbm,
    w_value_hbm,
    w_out_hbm,
    readout_hbm,
    out,
    coords,
    momenta,
    species,
    feats,
    nbr,
    ghost_rows,
    embed,
    w_filter,
    w_value,
    w_out,
    readout,
    sel,
    sel_t,
    handed,
    given,
    pos,
    text,
    halo0_out,
    halo0_in,
    halo1_out,
    halo1_in,
    grad_out,
    grad_in,
    pgrad_out,
    pgrad_in,
    state,
    kicked,
    momentum,
    offs,
    rads,
    apart,
    gv,
    p0,
    f1,
    f1_short,
    g1,
    h0,
    h1,
    u0,
    v1,
    back,
    parts,
    dh,
    dms,
    drs,
    dv,
    fown,
    halo_send,
    halo_recv,
    state_send,
    state_recv,
    kick_send,
    kick_recv,
    ready,
    fetch,
):
    beads, atoms = coords.shape[1:]
    ghosts = ghost_rows.shape[1] // 2
    channels = feats.shape[1]
    slots = nbr.shape[1]
    groups = slots // GROUP
    wide = GROUP * atoms
    me_b = lax.axis_index("bead")
    me_s = lax.axis_index("space")
    left = lax.rem(me_s + n_space - 1, n_space)
    right = lax.rem(me_s + 1, n_space)

    def signal(semaphore, offsets):
        for o in offsets:
            peer = lax.rem(me_b + (o % n_bead), n_bead)
            pl.semaphore_signal(semaphore, inc=1, device_id={"bead": peer}, device_id_type=MESH)

    fetched = dict(
        (name, pltpu.make_async_copy(source, here, fetch.at[i]))
        for i, (name, source, here) in enumerate(
            (
                ("feats", feats_hbm, feats),
                ("species", species_hbm, species),
                ("embed", embed_hbm, embed),
                ("w_value", w_value_hbm, w_value),
                ("ghost_rows", ghost_rows_hbm, ghost_rows),
                ("coords", coords_hbm, coords),
                ("nbr", nbr_hbm, nbr),
                ("w_filter", w_filter_hbm, w_filter),
                ("w_out", w_out_hbm, w_out),
                ("readout", readout_hbm, readout),
                ("momenta", momenta_hbm, momenta),
            )
        )
    )

    def fetch_done(*names):
        for name in names:
            fetched[name].wait()

    near, far_out = (1, -1, 8), (2, -2, 8)
    barrier = pltpu.get_barrier_semaphore()
    for side in (left, right):
        pl.semaphore_signal(barrier, inc=1, device_id={"space": side}, device_id_type=MESH)
    signal(barrier, near)
    for copy in fetched.values():
        copy.start()

    halos = ((halo0_out, halo0_in), (halo1_out, halo1_in), (grad_out, grad_in), (pgrad_out, pgrad_in))

    def halo(number, b):
        src, dst = halos[number]
        return [
            pltpu.make_async_remote_copy(
                src_ref=src.at[b, mine],
                dst_ref=dst.at[b, 1 - mine],
                send_sem=halo_send.at[number, b, mine],
                recv_sem=halo_recv.at[number, b, 1 - mine],
                device_id={"space": side},
                device_id_type=MESH,
            )
            for mine, side in enumerate((left, right))
        ]

    def to_beads(source, part, send, recv):
        return [
            pltpu.make_async_remote_copy(
                src_ref=source,
                dst_ref=part(o),
                send_sem=send.at[o],
                recv_sem=recv.at[o],
                device_id={"bead": lax.rem(me_b + o, n_bead)},
                device_id_type=MESH,
            )
            for o in outward
        ]

    half = n_bead // 2
    outward = sorted(range(1, n_bead), key=lambda o: -2 * min(o % half, half - o % half) - o // half)

    def states():
        return to_beads(coords, lambda o: state.at[o], state_send, state_recv)

    def kicks(b):
        return to_beads(kicked.at[0, b], lambda o: kicked.at[o, b], kick_send.at[b], kick_recv.at[b])

    def start_all(copies):
        for copy in copies:
            copy.start()

    def arrive(copies):
        for copy in copies:
            copy.wait_recv()

    fetch_done("feats", "species", "embed", "w_value", "ghost_rows", "coords")
    kinds = species[...]
    start = jnp.transpose(feats[...])
    mass = jnp.zeros((1, atoms), F32)
    for e in range(embed.shape[0]):
        column = jnp.transpose(jnp.broadcast_to(embed[e : e + 1, :], (128, channels)))
        column = jnp.concatenate([column] * (atoms // 128), axis=1)
        start = start + jnp.where(kinds == e, column, 0.0)
        mass = jnp.where(kinds == e, MASSES[e], mass)
    h0[...] = start
    hi, lo = split(start)
    wv0_t = jnp.transpose(w_value[0].astype(F32)).astype(BF16)
    values_zero = (dot(wv0_t, hi) + dot(wv0_t, lo)).astype(BF16)

    pos[...] = jnp.zeros_like(pos)
    for b in range(beads):
        for c in range(3):
            pos[b, c : c + 1, :] = coords[c, b : b + 1, :]
    atom_rows = lax.broadcasted_iota(jnp.int32, (atoms, atoms), 0).astype(F32).astype(BF16)
    atom_lanes = lax.broadcasted_iota(jnp.int32, (atoms, atoms), 1).astype(F32).astype(BF16)
    for b in range(beads):
        handed[b] = one_hot(ghost_rows[b : b + 1, :].astype(F32).astype(BF16), atom_rows)
        hi, lo = split(pos[b])
        table = jnp.concatenate([values_zero, hi, lo], axis=0)
        text[b] = table
        picked = dot(table, handed[b]).astype(BF16)
        halo0_out[b, 0] = picked[:, :ghosts]
        halo0_out[b, 1] = picked[:, ghosts:]

    pl.semaphore_wait(barrier, 2 + len(near))
    for b in range(beads):
        start_all(halo(0, b))
    signal(ready.at[0], near)

    fetch_done("nbr")
    for b in range(beads):
        lists = nbr[b].astype(F32)
        halves = [lists.astype(BF16), (lists - float(atoms)).astype(BF16)]
        for s in range(slots):
            here = slice(s * atoms, (s + 1) * atoms)
            for half, value in enumerate(halves):
                sel[b, half * atoms : (half + 1) * atoms, here] = one_hot(value[s : s + 1, :], atom_rows)
        got = dot(text[b], sel[b, :atoms, :])
        gv[b] = got[:channels]
        offs[b] = got[channels:]
    for b in range(beads):
        marks = jnp.broadcast_to(ghost_rows[b : b + 1, :], (8, 2 * ghosts))
        columns = jnp.transpose(jnp.concatenate([nbr[b], marks], axis=0)).astype(F32)
        given[b] = one_hot(columns[:, slots : slots + 1].astype(BF16), atom_lanes)
        for s in range(slots):
            here = slice(s * atoms, (s + 1) * atoms)
            column = jnp.broadcast_to(columns[:, s : s + 1], (atoms, atoms))
            sel_t[b, here, :atoms] = one_hot(column.astype(BF16), atom_lanes)
            sel_t[b, here, atoms:] = one_hot((column - float(atoms)).astype(BF16), atom_lanes)

    fetch_done("w_filter", "w_out", "readout", "momenta")
    def filter_rows(layer):
        hi, lo = split(jnp.transpose(w_filter[layer]))
        return jnp.concatenate([hi, hi, lo], axis=1)

    def transposed(weight):
        return jnp.transpose(weight.astype(F32)).astype(BF16)

    wf = [filter_rows(0), filter_rows(1)]
    wv1_t = transposed(w_value[1])
    wo_t = [transposed(w_out[0]), transposed(w_out[1])]
    read = jnp.transpose(jnp.broadcast_to(readout[...], (128, channels)))
    read = jnp.concatenate([read] * (atoms // 128), axis=1)
    momentum[...] = jnp.zeros_like(momentum)
    for b in range(beads):
        for c in range(3):
            momentum[b, c : c + 1, :] = momenta[c, b : b + 1, :]

    centers = SPACING * lax.broadcasted_iota(jnp.int32, (16, atoms), 0).astype(F32)
    lanes = [slice(s * atoms, (s + 1) * atoms) for s in range(slots)]
    chunks = [slice(g * wide, (g + 1) * wide) for g in range(groups)]

    def slope(x, gate):
        return gate * (1.0 + x * (1.0 - gate))

    def layer_zero(b):
        far = jnp.concatenate([halo0_in[b, 0], halo0_in[b, 1]], axis=1)
        for g in range(groups):
            here = chunks[g]
            got = dot(far, sel[b, atoms:, here])
            place = got[channels:] + offs[b, :, here]
            offs[b, 0:8, here] = place[0:8] + place[8:16]
            gv[b, :, here] = gv[b, :, here] + got[:channels]
        for here in lanes:
            off = offs[b, 0:8, here] - pos[b]
            offs[b, 0:8, here] = off
            square = jnp.sum(off * off, axis=0, keepdims=True) + SOFTEN
            inverse = lax.rsqrt(square)
            offs[b, 8:16, here] = jnp.broadcast_to(inverse, (8, atoms))
            t = square * inverse - centers
            apart[b, :, here] = t
            rads[b, :, here] = stacked(jnp.exp(-WIDTH * (t * t)))
        acc = jnp.zeros((channels, atoms), F32)
        for g in range(groups):
            weight = dot(wf[0], rads[b, :, chunks[g]])
            for s in range(GROUP):
                acc = acc + weight[:, lanes[s]] * gv[b, :, lanes[g * GROUP + s]]
        update = dot(wo_t[0], acc.astype(BF16))
        gate = jax.nn.sigmoid(update)
        u0[b] = slope(update, gate)
        hidden = h0[...] + update * gate
        h1[b] = hidden
        value = dot(wv1_t, hidden.astype(BF16)).astype(BF16)
        v1[b] = value
        picked = dot(value, handed[b]).astype(BF16)
        halo1_out[b, 0] = picked[:, :ghosts]
        halo1_out[b, 1] = picked[:, ghosts:]
        start_all(halo(1, b))

    def between(b):
        for g in range(groups):
            g1[b, :, chunks[g]] = dot(v1[b], sel[b, :atoms, chunks[g]])
        for here in lanes:
            weight = dot(wf[1], rads[b, :, here])
            f1[b, :, here] = weight
            f1_short[b, :, here] = weight.astype(BF16)

    def layer_one(b):
        far = jnp.concatenate([halo1_in[b, 0], halo1_in[b, 1]], axis=1)
        acc = jnp.zeros((channels, atoms), F32)
        for g in range(groups):
            got = dot(far, sel[b, atoms:, chunks[g]])
            for s in range(GROUP):
                here, there = lanes[g * GROUP + s], lanes[s]
                value = g1[b, :, here] + got[:, there]
                acc = acc + f1[b, :, here] * value
                g1[b, :, here] = value
        update = dot(wo_t[1], acc.astype(BF16))
        gate = jax.nn.sigmoid(update)
        hidden = h1[b] + update * gate
        grad = read * slope(hidden, jax.nn.sigmoid(hidden))
        dh[b] = grad
        grad = grad * slope(update, gate)
        message = dot(w_out[1], grad.astype(BF16))
        dms[b] = message
        short = message.astype(BF16)
        for here in lanes:
            back[b, :, here] = f1_short[b, :, here] * short
        value = dot(back[b], sel_t[b, :, atoms:]).astype(BF16)
        grad_out[b, 0] = value[:, :ghosts]
        grad_out[b, 1] = value[:, ghosts:]
        start_all(halo(2, b))

    def own_scatter(b):
        dv[b] = dot(back[b], sel_t[b, :, :atoms])
        for here in lanes:
            t = apart[b, :, here]
            steep = stacked((-2.0 * WIDTH) * (t * jnp.exp(-WIDTH * (t * t))))
            p0[b, :, here] = dot(wf[0], steep) * gv[b, :, here]
            change = dot(wf[1], steep) * g1[b, :, here]
            drs[b, :, here] = jnp.sum(dms[b] * change, axis=0, keepdims=True)

    def backward(b):
        arrived = jnp.concatenate([grad_in[b, 0], grad_in[b, 1]], axis=1)
        value = dv[b] + dot(arrived, given[b])
        grad = dh[b] + dot(w_value[1], value.astype(BF16))
        message = dot(w_out[0], (grad * u0[b]).astype(BF16))
        acc = jnp.zeros((8, atoms), F32)
        for here in lanes:
                slot = drs[b, :, here] + jnp.sum(message * p0[b, :, here], axis=0, keepdims=True)
                part = offs[b, 0:8, here] * offs[b, 8:16, here] * slot
                acc = acc + part
                parts[b, :, here] = jnp.concatenate(split(part), axis=0)
        total = dot(parts[b], sel_t[b, :, atoms:])
        total = total[0:8] + total[8:16]
        pgrad_out[b, 0] = total[:, :ghosts]
        pgrad_out[b, 1] = total[:, ghosts:]
        start_all(halo(3, b))
        total = dot(parts[b], sel_t[b, :, :atoms])
        fown[b] = total[0:8] + total[8:16] - acc

    def kick(b):
        arrived = jnp.concatenate([pgrad_in[b, 0], pgrad_in[b, 1]], axis=1)
        placed = dot(jnp.concatenate(split(arrived), axis=0), given[b])
        grad = fown[b] + placed[0:8] + placed[8:16]
        kicked[0, b] = momentum[b] - (0.5 * STEP_DT) * grad[0:4]
        start_all(kicks(b))

    arrive(halo(0, 0))
    pl.semaphore_wait(ready.at[0], len(near))
    signal(ready.at[1], far_out)
    layer_zero(0)
    arrive(halo(0, 1))
    layer_zero(1)
    between(0)
    pl.semaphore_wait(ready.at[1], len(far_out))
    start_all(states())
    between(1)
    arrive(halo(1, 0))
    layer_one(0)
    arrive(halo(1, 1))
    layer_one(1)
    own_scatter(0)
    own_scatter(1)
    arrive(halo(2, 0))
    backward(0)
    arrive(halo(2, 1))
    backward(1)

    keep, drift, spring = ring_tables(beads * n_bead)

    def of_positions(table):
        same = jnp.zeros((3, beads, atoms), F32)
        other = jnp.zeros((3, beads, atoms), F32)
        first = lax.broadcasted_iota(jnp.int32, (3, beads, atoms), 1) == 0
        count = len(table)
        for o in range(n_bead):
            source = coords[...] if o == 0 else state[o]
            same = same + table[(2 * o) % count] * source
            other = other + jnp.where(first, table[(2 * o + 1) % count], table[(2 * o - 1) % count]) * source
        return same + jnp.concatenate([other[:, 1:], other[:, :1]], axis=1)

    arrive(halo(3, 0))
    kick(0)
    arrive(halo(3, 1))
    kick(1)
    arrive(states())
    q_base = of_positions(keep)
    p_base = of_positions(spring)
    inverse_mass = 1.0 / mass
    sent = [states()] + [kicks(b) for b in range(beads)]
    sent += [halo(number, b) for number in range(len(halos)) for b in range(beads)]
    for copies in sent:
        for copy in copies:
            copy.wait_send()
    q_next = [jnp.zeros((4, atoms), F32)] * beads
    p_next = [jnp.zeros((4, atoms), F32)] * beads
    for c in range(beads):
        arrivals = kicks(c)
        for o in [0] + outward[::-1]:
            if o:
                arrivals[outward.index(o)].wait_recv()
            source = kicked[o, c]
            for b in range(beads):
                d = (beads * o + b - c) % len(keep)
                q_next[b] = q_next[b] + drift[d] * source
                p_next[b] = p_next[b] + keep[d] * source
    for b in range(beads):
        q_next[b] = q_next[b] * inverse_mass
        for c in range(3):
            out[0, c, b : b + 1, :] = q_base[c, b : b + 1] + q_next[b][c : c + 1, :]
            out[1, c, b : b + 1, :] = p_next[b][c : c + 1, :] - mass * p_base[c, b : b + 1]


def local(
    coords,
    momenta,
    species,
    atom_features,
    neighbours,
    ghost_rows,
    embed,
    w_filter,
    w_value,
    w_out,
    readout,
):
    n_bead, n_space = lax.axis_size("bead"), lax.axis_size("space")
    beads, _, atoms = coords.shape
    slots = neighbours.shape[2]
    ghosts = ghost_rows.shape[1] // 2
    channels = embed.shape[1]
    edges = slots * atoms
    rows = channels + 16
    vmem = pl.BlockSpec(memory_space=pltpu.VMEM)
    big = pltpu.VMEM((beads, channels, edges), F32)
    per_bead = pltpu.VMEM((beads, channels, atoms), F32)
    shape = jax.ShapeDtypeStruct((3, beads, atoms), F32)
    result = pl.pallas_call(
        functools.partial(kernel, n_bead, n_space),
        out_shape=pltpu.VMEM((2, 3, beads, atoms), F32),
        in_specs=[pl.BlockSpec(memory_space=pl.ANY)] * 11,
        out_specs=vmem,
        scratch_shapes=[
            pltpu.VMEM((3, beads, atoms), F32),
            pltpu.VMEM((3, beads, atoms), F32),
            pltpu.VMEM((1, atoms), jnp.int32),
            pltpu.VMEM(atom_features.shape, F32),
            pltpu.VMEM((beads, slots, atoms), jnp.int32),
            pltpu.VMEM(ghost_rows.shape, jnp.int32),
            pltpu.VMEM(embed.shape, F32),
            pltpu.VMEM(w_filter.shape, F32),
            pltpu.VMEM(w_value.shape, BF16),
            pltpu.VMEM(w_out.shape, BF16),
            pltpu.VMEM((1, channels), F32),
            pltpu.VMEM((beads, 2 * atoms, edges), BF16),
            pltpu.VMEM((beads, edges, 2 * atoms), BF16),
            pltpu.VMEM((beads, atoms, 2 * ghosts), BF16),
            pltpu.VMEM((beads, 2 * ghosts, atoms), BF16),
            pltpu.VMEM((beads, 8, atoms), F32),
            pltpu.VMEM((beads, rows, atoms), BF16),
            pltpu.VMEM((beads, 2, rows, ghosts), BF16),
            pltpu.VMEM((beads, 2, rows, ghosts), BF16),
            pltpu.VMEM((beads, 2, channels, ghosts), BF16),
            pltpu.VMEM((beads, 2, channels, ghosts), BF16),
            pltpu.VMEM((beads, 2, channels, ghosts), BF16),
            pltpu.VMEM((beads, 2, channels, ghosts), BF16),
            pltpu.VMEM((beads, 2, 8, ghosts), F32),
            pltpu.VMEM((beads, 2, 8, ghosts), F32),
            pltpu.VMEM((n_bead, 3, beads, atoms), F32),
            pltpu.VMEM((n_bead, beads, 4, atoms), F32),
            pltpu.VMEM((beads, 4, atoms), F32),
            pltpu.VMEM((beads, 16, edges), F32),
            pltpu.VMEM((beads, 48, edges), BF16),
            pltpu.VMEM((beads, 16, edges), F32),
            big,
            big,
            big,
            pltpu.VMEM((beads, channels, edges), BF16),
            big,
            pltpu.VMEM((channels, atoms), F32),
            per_bead,
            per_bead,
            pltpu.VMEM((beads, channels, atoms), BF16),
            pltpu.VMEM((beads, channels, edges), BF16),
            pltpu.VMEM((beads, 16, edges), BF16),
            per_bead,
            per_bead,
            pltpu.VMEM((beads, 1, edges), F32),
            per_bead,
            pltpu.VMEM((beads, 8, atoms), F32),
            pltpu.SemaphoreType.DMA((4, beads, 2)),
            pltpu.SemaphoreType.DMA((4, beads, 2)),
            pltpu.SemaphoreType.DMA((n_bead,)),
            pltpu.SemaphoreType.DMA((n_bead,)),
            pltpu.SemaphoreType.DMA((beads, n_bead)),
            pltpu.SemaphoreType.DMA((beads, n_bead)),
            pltpu.SemaphoreType.REGULAR((2,)),
            pltpu.SemaphoreType.DMA((11,)),
        ],
        compiler_params=pltpu.CompilerParams(
            collective_id=0, has_side_effects=True, vmem_limit_bytes=60 * 1024 * 1024
        ),
    )(
        jnp.transpose(coords, (1, 0, 2)),
        jnp.transpose(momenta, (1, 0, 2)),
        species.reshape(1, atoms),
        atom_features,
        jnp.transpose(neighbours, (0, 2, 1)),
        ghost_rows,
        embed,
        w_filter,
        w_value,
        w_out,
        readout.reshape(1, channels),
    )
    return jnp.transpose(result[0], (1, 0, 2)), jnp.transpose(result[1], (1, 0, 2))


def solution(mesh):
    placed = (
        P("bead", None, "space"),
        P("bead", None, "space"),
        P("space"),
        P("space", None),
        P("bead", "space", None),
        P("bead", "space"),
        P(),
        P(),
        P(),
        P(),
        P(),
    )
    return jax.shard_map(
        local,
        mesh=mesh,
        in_specs=placed,
        out_specs=(P("bead", None, "space"), P("bead", None, "space")),
        check_vma=False,
    )
```

```python
import functools
import math

import jax
import jax.numpy as jnp
from jax import lax
from jax.experimental import pallas as pl
from jax.experimental.pallas import tpu as pltpu
from jax.sharding import PartitionSpec as P

MASSES = (1.008, 12.011, 14.007, 15.999, 30.974)
STEP_DT = 1.0
OMEGA_P = 0.6
WIDTH = 3.125
SPACING = 0.25
SOFTEN = 0.01

MESH = pl.DeviceIdType.MESH
BF16 = jnp.bfloat16
F32 = jnp.float32
GROUP = 4


def dot(a, b):
    return jnp.dot(a, b, preferred_element_type=F32)


def one_hot(index, places):
    index = jnp.broadcast_to(index, places.shape)
    return jnp.where(index == places, jnp.ones(places.shape, BF16), jnp.zeros(places.shape, BF16))


def split(x):
    hi = x.astype(BF16)
    return hi, (x - hi.astype(F32)).astype(BF16)


def stacked(x):
    hi, lo = split(x)
    return jnp.concatenate([hi, lo, hi], axis=0)


def ring_tables(count):
    omegas = [2.0 * OMEGA_P * math.sin(math.pi * k / count) for k in range(count)]

    def kernel_of(g):
        return [
            sum(g(w) * math.cos(2.0 * math.pi * k * d / count) for k, w in enumerate(omegas)) / count
            for d in range(count)
        ]

    keep = kernel_of(lambda w: math.cos(w * STEP_DT))
    drift = kernel_of(lambda w: math.sin(w * STEP_DT) / w if w > 0.0 else STEP_DT)
    spring = kernel_of(lambda w: w * math.sin(w * STEP_DT))
    return keep, drift, spring


def kernel(
    n_bead,
    n_space,
    coords_hbm,
    momenta_hbm,
    species_hbm,
    feats_hbm,
    nbr_hbm,
    ghost_rows_hbm,
    embed_hbm,
    w_filter_hbm,
    w_value_hbm,
    w_out_hbm,
    readout_hbm,
    out,
    coords,
    momenta,
    species,
    feats,
    nbr,
    ghost_rows,
    embed,
    w_filter,
    w_value,
    w_out,
    readout,
    sel,
    sel_t,
    handed,
    given,
    pos,
    text,
    halo0_out,
    halo0_in,
    halo1_out,
    halo1_in,
    grad_out,
    grad_in,
    pgrad_out,
    pgrad_in,
    state,
    kicked,
    momentum,
    offs,
    rads,
    apart,
    gv,
    p0,
    f1,
    f1_short,
    g1,
    h0,
    h1,
    u0,
    v1,
    back,
    parts,
    dh,
    dms,
    drs,
    dv,
    fown,
    halo_send,
    halo_recv,
    state_send,
    state_recv,
    kick_send,
    kick_recv,
    ready,
    fetch,
):
    beads, atoms = coords.shape[1:]
    ghosts = ghost_rows.shape[1] // 2
    channels = feats.shape[1]
    slots = nbr.shape[1]
    groups = slots // GROUP
    wide = GROUP * atoms
    me_b = lax.axis_index("bead")
    me_s = lax.axis_index("space")
    left = lax.rem(me_s + n_space - 1, n_space)
    right = lax.rem(me_s + 1, n_space)

    def signal(semaphore, offsets):
        for o in offsets:
            peer = lax.rem(me_b + (o % n_bead), n_bead)
            pl.semaphore_signal(semaphore, inc=1, device_id={"bead": peer}, device_id_type=MESH)

    fetched = dict(
        (name, pltpu.make_async_copy(source, here, fetch.at[i]))
        for i, (name, source, here) in enumerate(
            (
                ("feats", feats_hbm, feats),
                ("species", species_hbm, species),
                ("embed", embed_hbm, embed),
                ("w_value", w_value_hbm, w_value),
                ("ghost_rows", ghost_rows_hbm, ghost_rows),
                ("coords", coords_hbm, coords),
                ("nbr", nbr_hbm, nbr),
                ("w_filter", w_filter_hbm, w_filter),
                ("w_out", w_out_hbm, w_out),
                ("readout", readout_hbm, readout),
                ("momenta", momenta_hbm, momenta),
            )
        )
    )

    def fetch_done(*names):
        for name in names:
            fetched[name].wait()

    near, far_out = (1, -1, 8), (2, -2, 8)
    barrier = pltpu.get_barrier_semaphore()
    for side in (left, right):
        pl.semaphore_signal(barrier, inc=1, device_id={"space": side}, device_id_type=MESH)
    signal(barrier, near)
    for copy in fetched.values():
        copy.start()

    halos = ((halo0_out, halo0_in), (halo1_out, halo1_in), (grad_out, grad_in), (pgrad_out, pgrad_in))

    def halo(number, b):
        src, dst = halos[number]
        return [
            pltpu.make_async_remote_copy(
                src_ref=src.at[b, mine],
                dst_ref=dst.at[b, 1 - mine],
                send_sem=halo_send.at[number, b, mine],
                recv_sem=halo_recv.at[number, b, 1 - mine],
                device_id={"space": side},
                device_id_type=MESH,
            )
            for mine, side in enumerate((left, right))
        ]

    def to_beads(source, part, send, recv):
        return [
            pltpu.make_async_remote_copy(
                src_ref=source,
                dst_ref=part(o),
                send_sem=send.at[o],
                recv_sem=recv.at[o],
                device_id={"bead": lax.rem(me_b + o, n_bead)},
                device_id_type=MESH,
            )
            for o in outward
        ]

    half = n_bead // 2
    outward = sorted(range(1, n_bead), key=lambda o: -2 * min(o % half, half - o % half) - o // half)

    def states():
        return to_beads(coords, lambda o: state.at[o], state_send, state_recv)

    def kicks(b):
        return to_beads(kicked.at[0, b], lambda o: kicked.at[o, b], kick_send.at[b], kick_recv.at[b])

    def start_all(copies):
        for copy in copies:
            copy.start()

    def arrive(copies):
        for copy in copies:
            copy.wait_recv()

    fetch_done("feats", "species", "embed", "w_value", "ghost_rows", "coords")
    kinds = species[...]
    start = jnp.transpose(feats[...])
    mass = jnp.zeros((1, atoms), F32)
    for e in range(embed.shape[0]):
        column = jnp.transpose(jnp.broadcast_to(embed[e : e + 1, :], (128, channels)))
        column = jnp.concatenate([column] * (atoms // 128), axis=1)
        start = start + jnp.where(kinds == e, column, 0.0)
        mass = jnp.where(kinds == e, MASSES[e], mass)
    h0[...] = start
    hi, lo = split(start)
    wv0_t = jnp.transpose(w_value[0].astype(F32)).astype(BF16)
    values_zero = (dot(wv0_t, hi) + dot(wv0_t, lo)).astype(BF16)

    pos[...] = jnp.zeros_like(pos)
    for b in range(beads):
        for c in range(3):
            pos[b, c : c + 1, :] = coords[c, b : b + 1, :]
    atom_rows = lax.broadcasted_iota(jnp.int32, (atoms, atoms), 0).astype(F32).astype(BF16)
    atom_lanes = lax.broadcasted_iota(jnp.int32, (atoms, atoms), 1).astype(F32).astype(BF16)
    for b in range(beads):
        handed[b] = one_hot(ghost_rows[b : b + 1, :].astype(F32).astype(BF16), atom_rows)
        hi, lo = split(pos[b])
        table = jnp.concatenate([values_zero, hi, lo], axis=0)
        text[b] = table
        picked = dot(table, handed[b]).astype(BF16)
        halo0_out[b, 0] = picked[:, :ghosts]
        halo0_out[b, 1] = picked[:, ghosts:]

    pl.semaphore_wait(barrier, 2 + len(near))
    for b in range(beads):
        start_all(halo(0, b))
    signal(ready.at[0], near)

    fetch_done("nbr")
    for b in range(beads):
        lists = nbr[b].astype(F32)
        halves = [lists.astype(BF16), (lists - float(atoms)).astype(BF16)]
        for s in range(slots):
            here = slice(s * atoms, (s + 1) * atoms)
            for half, value in enumerate(halves):
                sel[b, half * atoms : (half + 1) * atoms, here] = one_hot(value[s : s + 1, :], atom_rows)
        got = dot(text[b], sel[b, :atoms, :])
        gv[b] = got[:channels]
        offs[b] = got[channels:]
    for b in range(beads):
        marks = jnp.broadcast_to(ghost_rows[b : b + 1, :], (8, 2 * ghosts))
        columns = jnp.transpose(jnp.concatenate([nbr[b], marks], axis=0)).astype(F32)
        given[b] = one_hot(columns[:, slots : slots + 1].astype(BF16), atom_lanes)
        for s in range(slots):
            here = slice(s * atoms, (s + 1) * atoms)
            column = jnp.broadcast_to(columns[:, s : s + 1], (atoms, atoms))
            sel_t[b, here, :atoms] = one_hot(column.astype(BF16), atom_lanes)
            sel_t[b, here, atoms:] = one_hot((column - float(atoms)).astype(BF16), atom_lanes)

    fetch_done("w_filter", "w_out", "readout", "momenta")
    def filter_rows(layer):
        hi, lo = split(jnp.transpose(w_filter[layer]))
        return jnp.concatenate([hi, hi, lo], axis=1)

    def transposed(weight):
        return jnp.transpose(weight.astype(F32)).astype(BF16)

    wf = [filter_rows(0), filter_rows(1)]
    wv1_t = transposed(w_value[1])
    wo_t = [transposed(w_out[0]), transposed(w_out[1])]
    read = jnp.transpose(jnp.broadcast_to(readout[...], (128, channels)))
    read = jnp.concatenate([read] * (atoms // 128), axis=1)
    momentum[...] = jnp.zeros_like(momentum)
    for b in range(beads):
        for c in range(3):
            momentum[b, c : c + 1, :] = momenta[c, b : b + 1, :]

    centers = SPACING * lax.broadcasted_iota(jnp.int32, (16, atoms), 0).astype(F32)
    lanes = [slice(s * atoms, (s + 1) * atoms) for s in range(slots)]
    chunks = [slice(g * wide, (g + 1) * wide) for g in range(groups)]

    def slope(x, gate):
        return gate * (1.0 + x * (1.0 - gate))

    def layer_zero(b):
        far = jnp.concatenate([halo0_in[b, 0], halo0_in[b, 1]], axis=1)
        for g in range(groups):
            here = chunks[g]
            got = dot(far, sel[b, atoms:, here])
            place = got[channels:] + offs[b, :, here]
            offs[b, 0:8, here] = place[0:8] + place[8:16]
            gv[b, :, here] = gv[b, :, here] + got[:channels]
        for here in lanes:
            off = offs[b, 0:8, here] - pos[b]
            offs[b, 0:8, here] = off
            square = jnp.sum(off * off, axis=0, keepdims=True) + SOFTEN
            inverse = lax.rsqrt(square)
            offs[b, 8:16, here] = jnp.broadcast_to(inverse, (8, atoms))
            t = square * inverse - centers
            apart[b, :, here] = t
            rads[b, :, here] = stacked(jnp.exp(-WIDTH * (t * t)))
        acc = jnp.zeros((channels, atoms), F32)
        for g in range(groups):
            weight = dot(wf[0], rads[b, :, chunks[g]])
            for s in range(GROUP):
                acc = acc + weight[:, lanes[s]] * gv[b, :, lanes[g * GROUP + s]]
        update = dot(wo_t[0], acc.astype(BF16))
        gate = jax.nn.sigmoid(update)
        u0[b] = slope(update, gate)
        hidden = h0[...] + update * gate
        h1[b] = hidden
        value = dot(wv1_t, hidden.astype(BF16)).astype(BF16)
        v1[b] = value
        picked = dot(value, handed[b]).astype(BF16)
        halo1_out[b, 0] = picked[:, :ghosts]
        halo1_out[b, 1] = picked[:, ghosts:]
        start_all(halo(1, b))

    def between(b):
        for g in range(groups):
            g1[b, :, chunks[g]] = dot(v1[b], sel[b, :atoms, chunks[g]])
        for here in lanes:
            weight = dot(wf[1], rads[b, :, here])
            f1[b, :, here] = weight
            f1_short[b, :, here] = weight.astype(BF16)

    def layer_one(b):
        far = jnp.concatenate([halo1_in[b, 0], halo1_in[b, 1]], axis=1)
        acc = jnp.zeros((channels, atoms), F32)
        for g in range(groups):
            got = dot(far, sel[b, atoms:, chunks[g]])
            for s in range(GROUP):
                here, there = lanes[g * GROUP + s], lanes[s]
                value = g1[b, :, here] + got[:, there]
                acc = acc + f1[b, :, here] * value
                g1[b, :, here] = value
        update = dot(wo_t[1], acc.astype(BF16))
        gate = jax.nn.sigmoid(update)
        hidden = h1[b] + update * gate
        grad = read * slope(hidden, jax.nn.sigmoid(hidden))
        dh[b] = grad
        grad = grad * slope(update, gate)
        message = dot(w_out[1], grad.astype(BF16))
        dms[b] = message
        short = message.astype(BF16)
        for here in lanes:
            back[b, :, here] = f1_short[b, :, here] * short
        value = dot(back[b], sel_t[b, :, atoms:]).astype(BF16)
        grad_out[b, 0] = value[:, :ghosts]
        grad_out[b, 1] = value[:, ghosts:]
        start_all(halo(2, b))

    def own_scatter(b):
        dv[b] = dot(back[b], sel_t[b, :, :atoms])
        for here in lanes:
            t = apart[b, :, here]
            steep = stacked((-2.0 * WIDTH) * (t * jnp.exp(-WIDTH * (t * t))))
            p0[b, :, here] = dot(wf[0], steep) * gv[b, :, here]
            change = dot(wf[1], steep) * g1[b, :, here]
            drs[b, :, here] = jnp.sum(dms[b] * change, axis=0, keepdims=True)

    def backward(b):
        arrived = jnp.concatenate([grad_in[b, 0], grad_in[b, 1]], axis=1)
        value = dv[b] + dot(arrived, given[b])
        grad = dh[b] + dot(w_value[1], value.astype(BF16))
        message = dot(w_out[0], (grad * u0[b]).astype(BF16))
        acc = jnp.zeros((8, atoms), F32)
        for here in lanes:
                slot = drs[b, :, here] + jnp.sum(message * p0[b, :, here], axis=0, keepdims=True)
                part = offs[b, 0:8, here] * offs[b, 8:16, here] * slot
                acc = acc + part
                parts[b, :, here] = jnp.concatenate(split(part), axis=0)
        total = dot(parts[b], sel_t[b, :, atoms:])
        total = total[0:8] + total[8:16]
        pgrad_out[b, 0] = total[:, :ghosts]
        pgrad_out[b, 1] = total[:, ghosts:]
        start_all(halo(3, b))
        fown[b] = acc

    def own_positions(b):
        total = dot(parts[b], sel_t[b, :, :atoms])
        fown[b] = total[0:8] + total[8:16] - fown[b]

    def kick(b):
        arrived = jnp.concatenate([pgrad_in[b, 0], pgrad_in[b, 1]], axis=1)
        placed = dot(jnp.concatenate(split(arrived), axis=0), given[b])
        grad = fown[b] + placed[0:8] + placed[8:16]
        kicked[0, b] = momentum[b] - (0.5 * STEP_DT) * grad[0:4]
        start_all(kicks(b))

    arrive(halo(0, 0))
    pl.semaphore_wait(ready.at[0], len(near))
    signal(ready.at[1], far_out)
    layer_zero(0)
    arrive(halo(0, 1))
    layer_zero(1)
    between(0)
    pl.semaphore_wait(ready.at[1], len(far_out))
    start_all(states())
    between(1)
    arrive(halo(1, 0))
    layer_one(0)
    arrive(halo(1, 1))
    layer_one(1)
    own_scatter(0)
    own_scatter(1)
    arrive(halo(2, 0))
    backward(0)
    arrive(halo(2, 1))
    backward(1)
    own_positions(0)
    own_positions(1)

    keep, drift, spring = ring_tables(beads * n_bead)

    def of_positions(table):
        same = jnp.zeros((3, beads, atoms), F32)
        other = jnp.zeros((3, beads, atoms), F32)
        first = lax.broadcasted_iota(jnp.int32, (3, beads, atoms), 1) == 0
        count = len(table)
        for o in range(n_bead):
            source = coords[...] if o == 0 else state[o]
            same = same + table[(2 * o) % count] * source
            other = other + jnp.where(first, table[(2 * o + 1) % count], table[(2 * o - 1) % count]) * source
        return same + jnp.concatenate([other[:, 1:], other[:, :1]], axis=1)

    arrive(halo(3, 0))
    kick(0)
    arrive(halo(3, 1))
    kick(1)
    arrive(states())
    q_base = of_positions(keep)
    p_base = of_positions(spring)
    inverse_mass = 1.0 / mass
    sent = [states()] + [kicks(b) for b in range(beads)]
    sent += [halo(number, b) for number in range(len(halos)) for b in range(beads)]
    for copies in sent:
        for copy in copies:
            copy.wait_send()
    q_next = [jnp.zeros((4, atoms), F32)] * beads
    p_next = [jnp.zeros((4, atoms), F32)] * beads
    for c in range(beads):
        arrivals = kicks(c)
        for o in [0] + outward[::-1]:
            if o:
                arrivals[outward.index(o)].wait_recv()
            source = kicked[o, c]
            for b in range(beads):
                d = (beads * o + b - c) % len(keep)
                q_next[b] = q_next[b] + drift[d] * source
                p_next[b] = p_next[b] + keep[d] * source
    for b in range(beads):
        q_next[b] = q_next[b] * inverse_mass
        for c in range(3):
            out[0, c, b : b + 1, :] = q_base[c, b : b + 1] + q_next[b][c : c + 1, :]
            out[1, c, b : b + 1, :] = p_next[b][c : c + 1, :] - mass * p_base[c, b : b + 1]


def local(
    coords,
    momenta,
    species,
    atom_features,
    neighbours,
    ghost_rows,
    embed,
    w_filter,
    w_value,
    w_out,
    readout,
):
    n_bead, n_space = lax.axis_size("bead"), lax.axis_size("space")
    beads, _, atoms = coords.shape
    slots = neighbours.shape[2]
    ghosts = ghost_rows.shape[1] // 2
    channels = embed.shape[1]
    edges = slots * atoms
    rows = channels + 16
    vmem = pl.BlockSpec(memory_space=pltpu.VMEM)
    big = pltpu.VMEM((beads, channels, edges), F32)
    per_bead = pltpu.VMEM((beads, channels, atoms), F32)
    shape = jax.ShapeDtypeStruct((3, beads, atoms), F32)
    result = pl.pallas_call(
        functools.partial(kernel, n_bead, n_space),
        out_shape=pltpu.VMEM((2, 3, beads, atoms), F32),
        in_specs=[pl.BlockSpec(memory_space=pl.ANY)] * 11,
        out_specs=vmem,
        scratch_shapes=[
            pltpu.VMEM((3, beads, atoms), F32),
            pltpu.VMEM((3, beads, atoms), F32),
            pltpu.VMEM((1, atoms), jnp.int32),
            pltpu.VMEM(atom_features.shape, F32),
            pltpu.VMEM((beads, slots, atoms), jnp.int32),
            pltpu.VMEM(ghost_rows.shape, jnp.int32),
            pltpu.VMEM(embed.shape, F32),
            pltpu.VMEM(w_filter.shape, F32),
            pltpu.VMEM(w_value.shape, BF16),
            pltpu.VMEM(w_out.shape, BF16),
            pltpu.VMEM((1, channels), F32),
            pltpu.VMEM((beads, 2 * atoms, edges), BF16),
            pltpu.VMEM((beads, edges, 2 * atoms), BF16),
            pltpu.VMEM((beads, atoms, 2 * ghosts), BF16),
            pltpu.VMEM((beads, 2 * ghosts, atoms), BF16),
            pltpu.VMEM((beads, 8, atoms), F32),
            pltpu.VMEM((beads, rows, atoms), BF16),
            pltpu.VMEM((beads, 2, rows, ghosts), BF16),
            pltpu.VMEM((beads, 2, rows, ghosts), BF16),
            pltpu.VMEM((beads, 2, channels, ghosts), BF16),
            pltpu.VMEM((beads, 2, channels, ghosts), BF16),
            pltpu.VMEM((beads, 2, channels, ghosts), BF16),
            pltpu.VMEM((beads, 2, channels, ghosts), BF16),
            pltpu.VMEM((beads, 2, 8, ghosts), F32),
            pltpu.VMEM((beads, 2, 8, ghosts), F32),
            pltpu.VMEM((n_bead, 3, beads, atoms), F32),
            pltpu.VMEM((n_bead, beads, 4, atoms), F32),
            pltpu.VMEM((beads, 4, atoms), F32),
            pltpu.VMEM((beads, 16, edges), F32),
            pltpu.VMEM((beads, 48, edges), BF16),
            pltpu.VMEM((beads, 16, edges), F32),
            big,
            big,
            big,
            pltpu.VMEM((beads, channels, edges), BF16),
            big,
            pltpu.VMEM((channels, atoms), F32),
            per_bead,
            per_bead,
            pltpu.VMEM((beads, channels, atoms), BF16),
            pltpu.VMEM((beads, channels, edges), BF16),
            pltpu.VMEM((beads, 16, edges), BF16),
            per_bead,
            per_bead,
            pltpu.VMEM((beads, 1, edges), F32),
            per_bead,
            pltpu.VMEM((beads, 8, atoms), F32),
            pltpu.SemaphoreType.DMA((4, beads, 2)),
            pltpu.SemaphoreType.DMA((4, beads, 2)),
            pltpu.SemaphoreType.DMA((n_bead,)),
            pltpu.SemaphoreType.DMA((n_bead,)),
            pltpu.SemaphoreType.DMA((beads, n_bead)),
            pltpu.SemaphoreType.DMA((beads, n_bead)),
            pltpu.SemaphoreType.REGULAR((2,)),
            pltpu.SemaphoreType.DMA((11,)),
        ],
        compiler_params=pltpu.CompilerParams(
            collective_id=0, has_side_effects=True, vmem_limit_bytes=60 * 1024 * 1024
        ),
    )(
        jnp.transpose(coords, (1, 0, 2)),
        jnp.transpose(momenta, (1, 0, 2)),
        species.reshape(1, atoms),
        atom_features,
        jnp.transpose(neighbours, (0, 2, 1)),
        ghost_rows,
        embed,
        w_filter,
        w_value,
        w_out,
        readout.reshape(1, channels),
    )
    return jnp.transpose(result[0], (1, 0, 2)), jnp.transpose(result[1], (1, 0, 2))


def solution(mesh):
    placed = (
        P("bead", None, "space"),
        P("bead", None, "space"),
        P("space"),
        P("space", None),
        P("bead", "space", None),
        P("bead", "space"),
        P(),
        P(),
        P(),
        P(),
        P(),
    )
    return jax.shard_map(
        local,
        mesh=mesh,
        in_specs=placed,
        out_specs=(P("bead", None, "space"), P("bead", None, "space")),
        check_vma=False,
    )
```
